32 devices in a mesh: view: 4 (over y, x), row: 4 (over z), disp: 2 (over core).
Axes of the slice: x: 2, y: 2, z: 4, core: 2. Of those that a mesh axis runs over, the one named last changes fastest.
Arguments:
- images: float32 [4, 32, 2048], P('view', 'row')
- sharpness: float32 [4], P('view'), may hold values from 1 to 800
- paired: int32 [4, 2], P('view'), may hold values from 0 to 1, as said below
- offset: int32 [4, 2], P('view'), may hold values from 0 to 127
- row_range: int32 [4, 2, 2], P('view'), may hold values from 0 to 32, as said below
Outputs:
- left_disparity: float32 [4, 2, 32, 2048], P('view', None, 'row')
- right_disparity: float32 [4, 2, 32, 2048], P('view', None, 'row')
The draws below stay inside these ranges and needn't reach their ends.
Inputs may be any that keep to these rules, and one draw needn't show every extreme that they name: paired[v, j] is 0 whenever v + j + 1 >= 4. row_range[v, j, 0] <= 8 and row_range[v, j, 1] >= 24.
All inputs are finite; a program needn't handle non-finite values.
Results may differ from the reference program's by a relative error of at most 0.0003.
Values sent between devices are 32-bit elements; how exact they have to be, the bound alone decides.
A program may use at most 192 MiB of HBM per device.

```python
import math
import jax
import jax.numpy as jnp
from jax import lax

DISP = 256
RAD = 4
SLOTS = 2
OFFMAX = 128
COLS = 2048
VIEWS = 4
ROWS = 32


def draw_images(key, part):
    first_key, second_key, third_key = jax.random.split(key, 3)
    noise = jax.random.normal(first_key, (VIEWS, ROWS, COLS), jnp.float32)
    row_gain = jax.random.uniform(second_key, (VIEWS, ROWS, 1), jnp.float32, 0.0, 1.15)
    col_gain = jax.random.uniform(third_key, (VIEWS, 1, COLS), jnp.float32, 0.0, 1.15)
    contrast = jnp.exp(row_gain + col_gain)
    return noise * contrast


def draw_paired(key, part):
    coin_flips = jax.random.randint(key, (VIEWS, SLOTS), 0, 4)
    view_index = jnp.arange(VIEWS, dtype=jnp.int32)
    in_block = view_index[:, None] + jnp.arange(SLOTS, dtype=jnp.int32)[None, :] + 1 < VIEWS
    chosen = jax.random.randint(jax.random.fold_in(key, 1), (), 0, VIEWS - SLOTS)
    forced = view_index[:, None] == chosen
    active = ((coin_flips > 0) | forced) & in_block
    return active.astype(jnp.int32)


def draw_offset(key, part):
    shifts = jax.random.randint(key, (VIEWS * SLOTS,), 0, OFFMAX)
    ordering = jax.random.permutation(jax.random.fold_in(key, 2), VIEWS * SLOTS)
    shifts = shifts.at[ordering[0]].set(OFFMAX - 1).at[ordering[1]].set(0)
    return shifts.reshape(VIEWS, SLOTS)


def draw_row_range(key, part):
    quarter = ROWS // 4
    lower_row = jax.random.randint(key, (VIEWS * SLOTS,), 0, quarter + 1)
    upper_row = ROWS - jax.random.randint(jax.random.fold_in(key, 3), (VIEWS * SLOTS,), 0, quarter + 1)
    ordering = jax.random.permutation(jax.random.fold_in(key, 4), VIEWS * SLOTS)
    lower_row = lower_row.at[ordering[0]].set(0).reshape(VIEWS, SLOTS)
    upper_row = upper_row.at[ordering[1]].set(ROWS).reshape(VIEWS, SLOTS)
    return jnp.stack([lower_row, upper_row], axis=-1)


def level_of(rng, extent, cuts, low, high):
    level, own = 1.0, jax.random.fold_in(rng, 6)
    for position, blocks in cuts:
        heights = jnp.exp(jax.random.uniform(jax.random.fold_in(own, position), (blocks,), jnp.float32, low / len(cuts), high / len(cuts)))
        level = level * jnp.repeat(heights, extent[position] // blocks).reshape([-1 if axis == position else 1 for axis in range(len(extent))])
    return level


def setup_inputs(seed: int = 0) -> dict:
    streams_of = jax.random.split(jax.random.key(seed), 6)
    return {
        "images": draw_images(jax.random.fold_in(streams_of[5], 71), 0),
        "sharpness": jnp.clip(jnp.exp(math.log(800.0) - 6.684612 * jax.random.uniform(streams_of[1], (VIEWS,), jnp.float32) ** level_of(streams_of[1], (VIEWS,), ((0, 4),), -0.2, 0.2)), 1.0, 800.0),
        "paired": draw_paired(jax.random.fold_in(streams_of[5], 71), 0),
        "offset": draw_offset(jax.random.fold_in(streams_of[5], 71), 0),
        "row_range": draw_row_range(jax.random.fold_in(streams_of[5], 71), 0),
    }


EPSILON = 1e-05

def box_sum(field):
    row_count = field.shape[-2] - 2 * RAD
    col_count = field.shape[-1]
    running = field[..., 0:row_count, :]
    for offset_row in range(1, 2 * RAD + 1):
        running = running + field[..., offset_row:offset_row + row_count, :]
    widths = [(0, 0)] * (running.ndim - 1) + [(RAD, RAD)]
    padded = jnp.pad(running, widths)
    summed = padded[..., 0:col_count]
    for offset_col in range(1, 2 * RAD + 1):
        summed = summed + padded[..., offset_col:offset_col + col_count]
    return summed

def window_stats(rimmed):
    window = float((2 * RAD + 1) ** 2)
    center = box_sum(rimmed) / window
    spread = box_sum(rimmed * rimmed) / window - center * center
    return (center, spread)

def pair_disparity(left_image, right_image, shift_base, sharp_value):
    pad_cols = DISP + OFFMAX
    left_rim = jnp.pad(left_image, ((RAD, RAD), (0, 0)))
    right_rim = jnp.pad(right_image, ((RAD, RAD), (0, 0)))
    left_mean, left_var = window_stats(left_rim)
    right_mean, right_var = window_stats(right_rim)
    right_wide = jnp.pad(right_rim, ((0, 0), (pad_cols, 0)))
    mean_wide = jnp.pad(right_mean, ((0, 0), (pad_cols, 0)))
    var_wide = jnp.pad(right_var, ((0, 0), (pad_cols, 0)))
    column = jnp.arange(COLS, dtype=jnp.int32)
    window = float((2 * RAD + 1) ** 2)
    zero_index = jnp.zeros((), jnp.int32)

    def one_disparity(level):
        amount = (level + shift_base).astype(jnp.int32)
        start_col = (pad_cols - amount).astype(jnp.int32)
        moved_strip = lax.dynamic_slice(right_wide, (zero_index, start_col), (ROWS + 2 * RAD, COLS))
        cross_sum = box_sum(left_rim * moved_strip) / window
        moved_mean = lax.dynamic_slice(mean_wide, (zero_index, start_col), (ROWS, COLS))
        moved_var = lax.dynamic_slice(var_wide, (zero_index, start_col), (ROWS, COLS))
        ncc_left = (cross_sum - left_mean * moved_mean) * lax.rsqrt((left_var + EPSILON) * (moved_var + EPSILON))
        ncc_left = jnp.where(column[None, :] >= amount, ncc_left, -1.0)
        extended = jnp.pad(ncc_left, ((0, 0), (0, pad_cols)), constant_values=-1.0)
        ncc_right = lax.dynamic_slice(extended, (zero_index, amount), (ROWS, COLS))
        return (ncc_left, ncc_right)
    levels = jnp.arange(DISP, dtype=jnp.int32)
    ncc_left, ncc_right = lax.map(one_disparity, levels)
    values = levels.astype(ncc_left.dtype) / DISP
    results = []
    for volume in (ncc_left, ncc_right):
        weights = jax.nn.softmax(sharp_value * volume, axis=0)
        results.append(lax.optimization_barrier(jnp.sum(weights * values[:, None, None], axis=0)))
    return (results[0], results[1])

def reference(images, sharpness, paired, offset, row_range):
    row_index = jnp.arange(ROWS, dtype=jnp.int32)
    left_list = []
    right_list = []
    for slot_index in range(SLOTS):

        def per_view(view_index):
            partner = jnp.minimum(view_index + slot_index + 1, VIEWS - 1)
            return pair_disparity(images[view_index], images[partner], offset[view_index, slot_index], sharpness[view_index])
        left_slot, right_slot = lax.map(per_view, jnp.arange(VIEWS, dtype=jnp.int32))
        inside = (row_index[None, :] >= row_range[:, slot_index, 0:1]) & (row_index[None, :] < row_range[:, slot_index, 1:2])
        keeping = paired[:, slot_index].astype(left_slot.dtype)[:, None, None] * inside.astype(left_slot.dtype)[:, :, None]
        left_slot = left_slot * keeping
        right_slot = right_slot * keeping
        right_slot = jnp.concatenate([jnp.zeros((slot_index + 1, ROWS, COLS), left_slot.dtype), right_slot[:VIEWS - slot_index - 1]], axis=0)
        left_list.append(left_slot)
        right_list.append(right_slot)
    return (jnp.stack(left_list, axis=1), jnp.stack(right_list, axis=1))
```

```python
import functools
import math

import jax
import jax.numpy as jnp
from jax import lax
from jax.experimental import pallas as pl
from jax.experimental.pallas import tpu as pltpu
from jax.sharding import PartitionSpec as P

DISP = 256
RAD = 4
TAPS = 2 * RAD + 1
EPSILON = 1e-05
DEPTH = 256
PAD = 128
WIDTH = 512
BLOCK = 256
GRAIN = 16
MARGIN = 384
SPAN = 2 * BLOCK + GRAIN
HALF = 3 * 128 + GRAIN
EXTRA = DEPTH - GRAIN


def rounded(value):
    return value.astype(jnp.bfloat16).astype(jnp.float32)


def split3(value):
    high = rounded(value)
    middle = rounded(value - high)
    return (high, middle, value - high - middle)


def row_of(view, disp, row_count):
    group = lax.axis_size("view") * lax.axis_size("disp")
    return (view * lax.axis_size("disp") + disp) * row_count // group


def segments(row, row_count):
    found = []
    for delta in (-1, 0, 1):
        low = max(row - RAD, delta * row_count)
        high = min(row + RAD + 1, (delta + 1) * row_count)
        for begin, end in ((low, min(high, row + RAD)), (max(low, row + RAD), high)):
            if end > begin:
                found.append((delta, begin - delta * row_count, end - begin, begin - row + RAD))
    return found


def build(window_ref, left_cols, left_rows, right_cols, right_rows, gain):
    cols = left_cols.shape[1]
    sub = lax.broadcasted_iota(jnp.int32, (GRAIN, 128), 0)
    lane = lax.broadcasted_iota(jnp.int32, (GRAIN, DEPTH), 1) - EXTRA
    floor = [-part for part in split3(jnp.full((GRAIN, 128), gain, jnp.float32))]
    zero = jnp.zeros((GRAIN, 128), jnp.float32)
    left_mark, right_mark = (zero, zero)
    for place in range(3):
        left_mark = jnp.where(sub == 3 + place, floor[place], left_mark)
        right_mark = jnp.where(sub == 6 + place, 1.0, right_mark)
    floor = [-part for part in split3(jnp.full((GRAIN, DEPTH), gain, jnp.float32))]
    edge = jnp.zeros((GRAIN, DEPTH), jnp.float32)
    for place in range(6):
        edge = jnp.where(lane == 3 + place, floor[place % 3], edge)
    flag = jnp.where((lane >= 3) & (lane < 9), 1.0, 0.0).astype(jnp.bfloat16)
    left_rows[cols : cols + MARGIN, :] = jnp.concatenate([edge.astype(jnp.bfloat16)] * (MARGIN // GRAIN), axis=0)
    right_rows[0:MARGIN, :] = jnp.concatenate([flag] * (MARGIN // GRAIN), axis=0)
    wide = WIDTH // 128
    left_mark = jnp.concatenate([left_mark] * wide, axis=1)
    right_mark = jnp.concatenate([right_mark] * wide, axis=1)
    place = lax.broadcasted_iota(jnp.int32, (GRAIN, WIDTH), 0)

    def emit(values, end, order, mark, cols_ref, rows_ref, base, row_base):
        for index, value in enumerate(values):
            high = value.astype(jnp.bfloat16)
            parts = (high, (value - high.astype(jnp.float32)).astype(jnp.bfloat16))
            for group in range(3):
                start = (group * len(values) + index) * GRAIN
                cols_ref[start : start + GRAIN, pl.ds(base, WIDTH)] = parts[order[group]]
        high = rounded(end)
        parts = (high, end - high)
        rest = mark
        for group in range(3):
            rest = jnp.where(place == group, parts[order[group]], rest)
        cols_ref[EXTRA:DEPTH, pl.ds(base, WIDTH)] = rest.astype(jnp.bfloat16)
        rows_ref[pl.ds(row_base, WIDTH), :] = cols_ref[:, pl.ds(base, WIDTH)].T

    def body(step, carry):
        base = pl.multiple_of(step * WIDTH, WIDTH)
        main = window_ref[0:8, pl.ds(base, WIDTH + 2 * PAD)]
        last = window_ref[8:9, pl.ds(base, WIDTH + 2 * PAD)]
        taps = [main[:, PAD - RAD + tap : PAD - RAD + tap + WIDTH] for tap in range(TAPS)]
        fan = pltpu.roll(jnp.broadcast_to(last, (8, WIDTH + 2 * PAD)), 0, 1, stride=1, stride_axis=0)
        taps.append(fan[:, PAD - RAD + 7 : PAD - RAD + 7 + WIDTH])
        end = last[:, PAD + RAD : PAD + RAD + WIDTH]
        values = [jnp.concatenate(taps[index : index + 2], axis=0) for index in range(0, TAPS + 1, 2)]
        total = values[0]
        for value in values[1:]:
            total = total + value
        mean = (jnp.sum(total, axis=0, keepdims=True) + end) * (1.0 / (TAPS * TAPS))
        values = [value - mean for value in values]
        end = end - mean
        total = values[0] * values[0]
        for value in values[1:]:
            total = total + value * value
        var = (jnp.sum(total, axis=0, keepdims=True) + end * end) * (1.0 / (TAPS * TAPS))
        scale = lax.rsqrt(var + EPSILON) * (1.0 / TAPS)
        row_base = pl.multiple_of(MARGIN + base, 128)
        emit([value * scale for value in values], end * scale, (0, 0, 1), right_mark, right_cols, right_rows, base, row_base)
        scale = scale * gain
        emit([value * scale for value in values], end * scale, (0, 1, 0), left_mark, left_cols, left_rows, base, base)
        return carry

    lax.fori_loop(0, cols // WIDTH, body, 0)


def soft_half(score_ref, result_ref, column, skip, keep, left):
    lane = lax.broadcasted_iota(jnp.int32, (8, 128), 1)
    sub = lax.broadcasted_iota(jnp.int32, (8, 128), 0)
    skew = lane - sub
    sub_f = sub.astype(jnp.float32)
    lane_f = lane[0:1].astype(jnp.float32)
    slack = 0 if left else 1
    steps = DISP // 8
    corner = 128 // 8

    def load(step):
        return score_ref[pl.ds(8 * step + skip, 8), :]

    near = [skew < 8 * step + slack for step in range(corner)]
    scores = [jnp.where(near[step], load(step), load(step + steps)) for step in range(corner)]
    scores += [load(step) for step in range(corner, steps)]
    tops = scores[:4]
    for step in range(4, steps):
        tops[step % 4] = jnp.maximum(tops[step % 4], scores[step])
    top = jnp.maximum(jnp.maximum(tops[0], tops[1]), jnp.maximum(tops[2], tops[3]))
    top = jnp.broadcast_to(jnp.max(top, axis=0, keepdims=True), (8, 128))
    zero = jnp.zeros((8, 128), jnp.float32)
    summed, running, far = ([zero, zero], [zero, zero], [zero, zero])
    for step in range(steps):
        weight = jnp.exp2(scores[step] - top)
        if step < corner:
            far[step % 2] = far[step % 2] + jnp.where(near[step], 0.0, weight)
        summed[step % 2] = summed[step % 2] + weight
        running[step % 2] = running[step % 2] + summed[step % 2]
    both = summed[0] + summed[1]
    moment = 8.0 * (steps * both - 2.0 * (running[0] + running[1]) + summed[1])
    moment = moment + sub_f * both + float(DISP) * (far[0] + far[1])
    total = jnp.sum(both, axis=0, keepdims=True)
    moment = jnp.sum(moment, axis=0, keepdims=True)
    if left:
        weighted = (lane_f + DISP) * total - moment
    else:
        weighted = moment - lane_f * total
    result_ref[:, pl.ds(column, 128)] = weighted * keep / (total * DISP)


def soft_pair(left_cols, left_rows, right_cols, right_rows, left_score, right_score, left_result, right_result, coarse, fine, keep):
    cols = left_cols.shape[1]
    count = cols // BLOCK

    def scores(rows_ref, row_start, cols_ref, block, score_ref):
        score = jnp.dot(
            rows_ref[pl.ds(row_start * GRAIN, SPAN), :],
            cols_ref[:, pl.ds(pl.multiple_of(block * BLOCK, BLOCK), BLOCK)],
            preferred_element_type=jnp.float32,
        )
        score_ref[0] = score[0:HALF, 0:128]
        score_ref[1] = score[128 : 128 + HALF, 128:256]

    def left_scores(block):
        scores(right_rows, block * (BLOCK // GRAIN) + (MARGIN - BLOCK - GRAIN) // GRAIN - coarse, left_cols, block, left_score)

    def right_scores(block):
        scores(left_rows, block * (BLOCK // GRAIN) + coarse, right_cols, block, right_score)

    def soft(score_ref, result_ref, block, skip, left):
        for half in range(2):
            column = pl.multiple_of(block * BLOCK + half * 128, 128)
            soft_half(score_ref.at[half], result_ref, column, skip, keep, left)

    def body(block, carry):
        right_scores(block)
        soft(left_score, left_result, block, GRAIN - fine, True)
        left_scores(jnp.minimum(block + 1, count - 1))
        soft(right_score, right_result, block, fine, False)
        return carry

    left_scores(0)
    lax.fori_loop(0, count, body, 0, unroll=2)


def place_of(view, row, disp):
    return dict(device_id={"view": view, "row": row, "disp": disp}, device_id_type=pl.DeviceIdType.MESH)


def signal(view, row, disp):
    pl.semaphore_signal(pltpu.get_barrier_semaphore(), inc=1, **place_of(view, row, disp))


def match_kernel(
    slots, image_ref, sharp_ref, paired_ref, offset_ref, range_ref, left_ref, right_ref,
    window, ints, floats, int_table, float_table,
    left_cols, left_rows, right_cols, right_rows, left_score, right_score, result,
    window_send, window_recv, meta_send, meta_recv, table_sem, result_send, result_recv,
):
    count, cols = image_ref.shape
    views, bands, disps = (lax.axis_size(axis) for axis in ("view", "row", "disp"))
    view, band, disp = (lax.axis_index(axis) for axis in ("view", "row", "disp"))
    group = views * disps
    share = group // count
    member = view * disps + disp
    mine = row_of(view, disp, count)
    sends = member % share == 0
    rows_of = [sorted({row_of(other, place, count) for place in range(disps)}) for other in range(views)]

    window[...] = jnp.zeros_like(window)
    left_ref[...] = jnp.zeros_like(left_ref)
    right_ref[...] = jnp.zeros_like(right_ref)
    for slot in range(slots):

        def fill(kind, value):
            ints[view, kind * slots + slot : kind * slots + slot + 1] = value

        shift = jnp.full((1, 128), offset_ref[0, slot], jnp.int32)
        fill(0, jnp.full((1, 128), paired_ref[0, slot], jnp.int32))
        fill(1, shift >> GRAIN.bit_length() - 1)
        fill(2, shift & (GRAIN - 1))
        for end in range(2):
            fill(3 + end, jnp.full((1, 128), range_ref[0, slot, end], jnp.int32))
    floats[view] = jnp.full((8, 128), sharp_ref[0], jnp.float32)

    def inside(row):
        return (row >= 0) & (row < bands)

    for other in range(views):
        for place in range(disps):

            @pl.when((view != other) | (disp != place))
            def _():
                signal(other, band, place)

    expected = group - 1
    for delta in (-1, 1):
        needs = False
        wanted = 0
        for row in range(count):
            has = any(part[0] == delta for part in segments(row, count))
            needs = needs | ((mine == row) & has)
        for other in range(views):
            for row in rows_of[other]:
                if any(part[0] == delta for part in segments(row, count)):
                    wanted = wanted + jnp.where(row_of(other, disp, count) == row, 1, 0)

        @pl.when(needs & inside(band + delta))
        def _():
            for other in range(views):
                signal(other, band + delta, disp)

        expected = expected + jnp.where(inside(band - delta), wanted, 0)
    pl.semaphore_wait(pltpu.get_barrier_semaphore(), expected)

    def window_copy(source, part, index, other, target_band):
        delta, begin, length, place = part
        return pltpu.make_async_remote_copy(
            src_ref=image_ref.at[pl.ds(begin, length)],
            dst_ref=window.at[source, pl.ds(place, length), pl.ds(PAD, cols)],
            send_sem=window_send.at[other, index],
            recv_sem=window_recv.at[source, index],
            **place_of(other, target_band, disp),
        )

    def own_copy(part, index):
        delta, begin, length, place = part
        return pltpu.make_async_copy(
            image_ref.at[pl.ds(begin, length)],
            window.at[view, pl.ds(place, length), pl.ds(PAD, cols)],
            window_recv.at[view, index],
        )

    def meta_copies(source, other):
        return [
            pltpu.make_async_remote_copy(
                src_ref=ref.at[source], dst_ref=ref.at[source],
                send_sem=meta_send.at[other, index], recv_sem=meta_recv.at[source, index],
                **place_of(other, band, disp),
            )
            for index, ref in enumerate((ints, floats))
        ]

    def sending(step, local):
        for other in range(views):

            @pl.when(view != other)
            def _():
                for copy in meta_copies(view, other):
                    step(copy)

            for row in rows_of[other]:
                aimed = row_of(other, disp, count) == row
                for index, part in enumerate(segments(row, count)):
                    if part[0] == 0:

                        @pl.when(aimed & (view != other))
                        def _():
                            step(window_copy(view, part, index, other, band))

                        if local:

                            @pl.when(aimed & (view == other))
                            def _():
                                own_copy(part, index).start()

                    else:

                        @pl.when(aimed & inside(band - part[0]))
                        def _():
                            step(window_copy(view, part, index, other, band - part[0]))

    sending(lambda copy: copy.start(), True)

    for other in range(views):

        @pl.when(view != other)
        def _():
            for copy in meta_copies(other, other):
                copy.wait_recv()

    tables = [
        pltpu.make_async_copy(ints, int_table, table_sem.at[0]),
        pltpu.make_async_copy(floats, float_table, table_sem.at[1]),
    ]
    for copy in tables:
        copy.start()
    for copy in tables:
        copy.wait()

    def arrive(source):
        for row in range(count):
            for index, part in enumerate(segments(row, count)):
                if part[0] == 0:

                    @pl.when((mine == row) & (view != source))
                    def _():
                        window_copy(source, part, index, source, band).wait_recv()

                    @pl.when((mine == row) & (view == source))
                    def _():
                        own_copy(part, index).wait()

                else:

                    @pl.when((mine == row) & inside(band + part[0]))
                    def _():
                        window_copy(source, part, index, source, band + part[0]).wait_recv()

    for source in range(views):
        arrive(source)

    def build_view(source, carry):
        build(
            window.at[source], left_cols.at[source], left_rows.at[source], right_cols.at[source], right_rows.at[source],
            float_table[source, 0, 0] * math.log2(math.e),
        )
        return carry

    lax.fori_loop(0, views, build_view, 0)

    pairs = [(first, slot) for first in range(views - 1) for slot in range(min(slots, views - 1 - first))]

    def outcome(index, first, slot, side, place):
        target = first + side * (slot + 1)
        out = (left_ref, right_ref)[side].at[slot, pl.ds(mine, 1)]
        source = result.at[index, side]
        away = lambda: pltpu.make_async_remote_copy(
            src_ref=source, dst_ref=out,
            send_sem=result_send.at[index, side, place], recv_sem=result_recv.at[mine, side, slot],
            **place_of(target, band, place),
        )
        home = lambda: pltpu.make_async_copy(source, out, result_recv.at[mine, side, slot])
        return target, (away, home)

    def spread(index, first, slot, start):
        for side in range(2):
            for place in range(disps):
                target, (away, home) = outcome(index, first, slot, side, place)
                own = (target == view) & (disp == place)

                @pl.when(sends & jnp.logical_not(own))
                def _():
                    if start:
                        away().start()
                    else:
                        away().wait_send()

                if start:

                    @pl.when(sends & own)
                    def _():
                        home().start()

    def find(index):
        first = sum(jnp.where(index == at, pair[0], 0) for at, pair in enumerate(pairs))
        slot = sum(jnp.where(index == at, pair[1], 0) for at, pair in enumerate(pairs))
        return first, slot

    line = band * count + mine

    def match_pair(index, carry):
        first, slot = find(index)
        partner = first + slot + 1
        begin, end, pairing = (ints[first, pl.ds(kind * slots + slot, 1), :] for kind in (3, 4, 0))
        keep = jnp.where((begin <= line) & (end > line), pairing, 0).astype(jnp.float32)
        soft_pair(
            left_cols.at[first], left_rows.at[first], right_cols.at[partner], right_rows.at[partner],
            left_score, right_score, result.at[index, 0], result.at[index, 1],
            int_table[first, slots + slot, 0], int_table[first, 2 * slots + slot, 0], keep,
        )
        spread(index, first, slot, True)
        return carry

    lax.fori_loop(0, len(pairs), match_pair, 0)

    for row in range(count):
        own = member == row * share
        for side in range(2):
            for slot in range(slots):
                other = view + slot + 1 if side == 0 else view - slot - 1
                exists = (other >= 0) & (other < views)
                out = (left_ref, right_ref)[side].at[slot, pl.ds(row, 1)]
                source = result.at[0, side]

                @pl.when(exists & jnp.logical_not(own))
                def _():
                    pltpu.make_async_remote_copy(
                        src_ref=source, dst_ref=out,
                        send_sem=result_send.at[0, side, 0], recv_sem=result_recv.at[row, side, slot],
                        **place_of(row * share // disps, band, row * share % disps),
                    ).wait_recv()

                @pl.when(exists & own)
                def _():
                    pltpu.make_async_copy(source, out, result_recv.at[row, side, slot]).wait()

    sending(lambda copy: copy.wait_send(), False)
    for index, (first, slot) in enumerate(pairs):
        spread(index, first, slot, False)


def match(image, sharpness, paired, offset, row_range):
    views, disps = (lax.axis_size(axis) for axis in ("view", "disp"))
    count, cols = image.shape
    slots = paired.shape[1]
    pairs = sum(min(slots, views - 1 - first) for first in range(views - 1))
    entries = -(-5 * slots // 8) * 8
    smem = pl.BlockSpec(memory_space=pltpu.SMEM)
    vmem = pl.BlockSpec(memory_space=pltpu.VMEM)
    out = jax.ShapeDtypeStruct((slots, count, cols), jnp.float32)
    dma = pltpu.SemaphoreType.DMA
    return pl.pallas_call(
        functools.partial(match_kernel, slots),
        out_shape=(out, out),
        in_specs=[vmem, smem, smem, smem, smem],
        out_specs=(vmem, vmem),
        scratch_shapes=[
            pltpu.VMEM((views, 16, cols + 2 * PAD), jnp.float32),
            pltpu.VMEM((views, entries, 128), jnp.int32),
            pltpu.VMEM((views, 8, 128), jnp.float32),
            pltpu.SMEM((views, entries, 128), jnp.int32),
            pltpu.SMEM((views, 8, 128), jnp.float32),
            pltpu.VMEM((views, DEPTH, cols), jnp.bfloat16),
            pltpu.VMEM((views, cols + MARGIN, DEPTH), jnp.bfloat16),
            pltpu.VMEM((views, DEPTH, cols), jnp.bfloat16),
            pltpu.VMEM((views, cols + MARGIN, DEPTH), jnp.bfloat16),
            pltpu.VMEM((2, HALF, 128), jnp.float32),
            pltpu.VMEM((2, HALF, 128), jnp.float32),
            pltpu.VMEM((pairs, 2, 1, cols), jnp.float32),
            dma((views, 3)),
            dma((views, 3)),
            dma((views, 2)),
            dma((views, 2)),
            dma((2,)),
            dma((pairs, 2, disps)),
            dma((count, 2, slots)),
        ],
        compiler_params=pltpu.CompilerParams(
            collective_id=0, has_side_effects=True, vmem_limit_bytes=40 * 1024 * 1024
        ),
        name="match",
    )(image, sharpness, paired, offset, row_range)


def shards(images, sharpness, paired, offset, row_range):
    left, right = match(images[0], sharpness, paired, offset, row_range)
    return (left[None], right[None])


def solution(mesh):
    return jax.shard_map(
        shards,
        mesh=mesh,
        in_specs=(
            P("view", "row", None),
            P("view"),
            P("view", None),
            P("view", None),
            P("view", None, None),
        ),
        out_specs=(P("view", None, "row", None), P("view", None, "row", None)),
        check_vma=False,
    )
```

```python
import functools
import math

import jax
import jax.numpy as jnp
from jax import lax
from jax.experimental import pallas as pl
from jax.experimental.pallas import tpu as pltpu
from jax.sharding import PartitionSpec as P

DISP = 256
RAD = 4
TAPS = 2 * RAD + 1
EPSILON = 1e-05
DEPTH = 256
PAD = 128
BLOCK = 256
GRAIN = 16
MARGIN = 384
SPAN = 2 * BLOCK + GRAIN
HALF = 3 * 128 + GRAIN
EXTRA = DEPTH - GRAIN


def rounded(value):
    return value.astype(jnp.bfloat16).astype(jnp.float32)


def split3(value):
    high = rounded(value)
    middle = rounded(value - high)
    return (high, middle, value - high - middle)


def row_of(view, disp, row_count):
    group = lax.axis_size("view") * lax.axis_size("disp")
    return (view * lax.axis_size("disp") + disp) * row_count // group


def segments(row, row_count):
    found = []
    for delta in (-1, 0, 1):
        low = max(row - RAD, delta * row_count)
        high = min(row + RAD + 1, (delta + 1) * row_count)
        for begin, end in ((low, min(high, row + RAD)), (max(low, row + RAD), high)):
            if end > begin:
                found.append((delta, begin - delta * row_count, end - begin, begin - row + RAD))
    return found


def tiled(row, width):
    return jnp.concatenate([row] * (width // 128), axis=1)


def emit(values, end, order, mark, cols_ref):
    for index, value in enumerate(values):
        high = value.astype(jnp.bfloat16)
        parts = (high, (value - high.astype(jnp.float32)).astype(jnp.bfloat16))
        for group in range(3):
            start = (group * len(values) + index) * GRAIN
            cols_ref[start : start + GRAIN, :] = parts[order[group]]
    high = rounded(end)
    parts = (high, end - high)
    place = lax.broadcasted_iota(jnp.int32, (GRAIN, end.shape[1]), 0)
    rest = mark
    for group in range(3):
        rest = jnp.where(place == group, parts[order[group]], rest)
    cols_ref[EXTRA:DEPTH, :] = rest.astype(jnp.bfloat16)


def build(window_ref, gain, left_refs, right_refs):
    cols = window_ref.shape[1] - 2 * PAD
    sub = lax.broadcasted_iota(jnp.int32, (GRAIN, 128), 0)
    lane = lax.broadcasted_iota(jnp.int32, (GRAIN, DEPTH), 1) - EXTRA
    main = window_ref[0:8, :]
    last = window_ref[8:9, :]
    taps = [main[:, PAD - RAD + tap : PAD - RAD + tap + cols] for tap in range(TAPS)]
    fan = pltpu.roll(jnp.broadcast_to(last, main.shape), 0, 1, stride=1, stride_axis=0)
    taps.append(fan[:, PAD - RAD + 7 : PAD - RAD + 7 + cols])
    end = last[:, PAD + RAD : PAD + RAD + cols]
    values = [jnp.concatenate(taps[index : index + 2], axis=0) for index in range(0, TAPS + 1, 2)]
    total = values[0]
    for value in values[1:]:
        total = total + value
    mean = (jnp.sum(total, axis=0, keepdims=True) + end) * (1.0 / (TAPS * TAPS))
    values = [value - mean for value in values]
    end = end - mean
    total = values[0] * values[0]
    for value in values[1:]:
        total = total + value * value
    var = (jnp.sum(total, axis=0, keepdims=True) + end * end) * (1.0 / (TAPS * TAPS))
    scale = lax.rsqrt(var + EPSILON) * (1.0 / TAPS)
    zero = jnp.zeros((GRAIN, 128), jnp.float32)
    if right_refs is not None:
        cols_ref, rows_ref = right_refs
        mark = jnp.where((sub >= 6) & (sub < 9), 1.0, zero)
        emit([value * scale for value in values], end * scale, (0, 0, 1), tiled(mark, cols), cols_ref)
        rows_ref[MARGIN : MARGIN + cols, :] = cols_ref[...].T
        flag = jnp.where((lane >= 3) & (lane < 9), 1.0, 0.0).astype(jnp.bfloat16)
        rows_ref[0:MARGIN, :] = jnp.concatenate([flag] * (MARGIN // GRAIN), axis=0)
    if left_refs is not None:
        cols_ref, rows_ref = left_refs
        floor = [-part for part in split3(jnp.broadcast_to(gain, (GRAIN, 128)))]
        mark = zero
        for place in range(3):
            mark = jnp.where(sub == 3 + place, floor[place], mark)
        scale = scale * tiled(gain, cols)
        emit([value * scale for value in values], end * scale, (0, 1, 0), tiled(mark, cols), cols_ref)
        rows_ref[0:cols, :] = cols_ref[...].T
        edge = jnp.zeros((GRAIN, DEPTH), jnp.float32)
        for place in range(6):
            edge = jnp.where(lane == 3 + place, tiled(floor[place % 3], DEPTH), edge)
        rows_ref[cols : cols + MARGIN, :] = jnp.concatenate([edge.astype(jnp.bfloat16)] * (MARGIN // GRAIN), axis=0)


def soft_half(score_ref, result_ref, column, skip, keep, left):
    lane = lax.broadcasted_iota(jnp.int32, (8, 128), 1)
    sub = lax.broadcasted_iota(jnp.int32, (8, 128), 0)
    skew = lane - sub
    sub_f = sub.astype(jnp.float32)
    lane_f = lane[0:1].astype(jnp.float32)
    slack = 0 if left else 1
    steps = DISP // 8
    corner = 128 // 8

    def load(step):
        return score_ref[pl.ds(8 * step + skip, 8), :]

    near = [skew < 8 * step + slack for step in range(corner)]
    scores = [jnp.where(near[step], load(step), load(step + steps)) for step in range(corner)]
    scores += [load(step) for step in range(corner, steps)]
    tops = scores[:4]
    for step in range(4, steps):
        tops[step % 4] = jnp.maximum(tops[step % 4], scores[step])
    top = jnp.maximum(jnp.maximum(tops[0], tops[1]), jnp.maximum(tops[2], tops[3]))
    top = jnp.broadcast_to(jnp.max(top, axis=0, keepdims=True), (8, 128))
    zero = jnp.zeros((8, 128), jnp.float32)
    summed, running, far = ([zero, zero], [zero, zero], [zero, zero])
    for step in range(steps):
        weight = jnp.exp2(scores[step] - top)
        if step < corner:
            far[step % 2] = far[step % 2] + jnp.where(near[step], 0.0, weight)
        summed[step % 2] = summed[step % 2] + weight
        running[step % 2] = running[step % 2] + summed[step % 2]
    both = summed[0] + summed[1]
    moment = 8.0 * (steps * both - 2.0 * (running[0] + running[1]) + summed[1])
    moment = moment + sub_f * both + float(DISP) * (far[0] + far[1])
    total = jnp.sum(both, axis=0, keepdims=True)
    moment = jnp.sum(moment, axis=0, keepdims=True)
    if left:
        weighted = (lane_f + DISP) * total - moment
    else:
        weighted = moment - lane_f * total
    result_ref[:, pl.ds(column, 128)] = weighted * keep / (total * DISP)


def soft_pair(left_cols, left_rows, right_cols, right_rows, left_score, right_score, left_result, right_result, coarse, fine, keep):
    cols = left_cols.shape[1]
    count = cols // BLOCK

    def scores(rows_ref, row_start, cols_ref, block, score_ref):
        score = jnp.dot(
            rows_ref[pl.ds(row_start * GRAIN, SPAN), :],
            cols_ref[:, pl.ds(pl.multiple_of(block * BLOCK, BLOCK), BLOCK)],
            preferred_element_type=jnp.float32,
        )
        score_ref[0] = score[0:HALF, 0:128]
        score_ref[1] = score[128 : 128 + HALF, 128:256]

    def left_scores(block):
        scores(right_rows, block * (BLOCK // GRAIN) + (MARGIN - BLOCK - GRAIN) // GRAIN - coarse, left_cols, block, left_score)

    def right_scores(block):
        scores(left_rows, block * (BLOCK // GRAIN) + coarse, right_cols, block, right_score)

    def soft(score_ref, result_ref, block, skip, left):
        for half in range(2):
            column = pl.multiple_of(block * BLOCK + half * 128, 128)
            soft_half(score_ref.at[half], result_ref, column, skip, keep, left)

    def body(block, carry):
        right_scores(block)
        soft(left_score, left_result, block, GRAIN - fine, True)
        left_scores(jnp.minimum(block + 1, count - 1))
        soft(right_score, right_result, block, fine, False)
        return carry

    left_scores(0)
    lax.fori_loop(0, count, body, 0, unroll=True)


def place_of(view, row, disp):
    return dict(device_id={"view": view, "row": row, "disp": disp}, device_id_type=pl.DeviceIdType.MESH)


def signal(view, row, disp):
    pl.semaphore_signal(pltpu.get_barrier_semaphore(), inc=1, **place_of(view, row, disp))


def match_kernel(
    slots, image_ref, sharp_hbm, paired_hbm, offset_hbm, range_hbm, left_ref, right_ref,
    sharp_ref, paired_ref, offset_ref, range_ref, window, ints, floats, int_table,
    left_cols, left_rows, right_cols, right_rows, left_score, right_score, result,
    window_send, window_recv, meta_send, meta_recv, scalar_sem, table_sem, result_send, result_recv,
):
    count, cols = image_ref.shape
    views, bands, disps = (lax.axis_size(axis) for axis in ("view", "row", "disp"))
    view, band, disp = (lax.axis_index(axis) for axis in ("view", "row", "disp"))
    group = views * disps
    share = group // count
    member = view * disps + disp
    mine = row_of(view, disp, count)
    sends = member % share == 0
    rows_of = [sorted({row_of(other, place, count) for place in range(disps)}) for other in range(views)]

    scalars = [
        pltpu.make_async_copy(source, target, scalar_sem.at[index])
        for index, (source, target) in enumerate(
            ((sharp_hbm, sharp_ref), (paired_hbm, paired_ref), (offset_hbm, offset_ref), (range_hbm, range_ref))
        )
    ]
    for copy in scalars:
        copy.start()
    window[...] = jnp.zeros_like(window)
    left_ref[...] = jnp.zeros_like(left_ref)
    right_ref[...] = jnp.zeros_like(right_ref)

    def inside(row):
        return (row >= 0) & (row < bands)

    for other in range(views):
        for place in range(disps):

            @pl.when((view != other) | (disp != place))
            def _():
                signal(other, band, place)

    expected = group - 1
    for delta in (-1, 1):
        needs = False
        wanted = 0
        for row in range(count):
            has = any(part[0] == delta for part in segments(row, count))
            needs = needs | ((mine == row) & has)
        for other in range(views):
            for row in rows_of[other]:
                if any(part[0] == delta for part in segments(row, count)):
                    wanted = wanted + jnp.where(row_of(other, disp, count) == row, 1, 0)

        @pl.when(needs & inside(band + delta))
        def _():
            for other in range(views):
                signal(other, band + delta, disp)

        expected = expected + jnp.where(inside(band - delta), wanted, 0)
    for copy in scalars:
        copy.wait()
    for slot in range(slots):

        def fill(kind, value):
            ints[view, kind * slots + slot : kind * slots + slot + 1] = value

        shift = jnp.broadcast_to(offset_ref[0:1, slot : slot + 1], (1, 128))
        fill(0, jnp.broadcast_to(paired_ref[0:1, slot : slot + 1], (1, 128)))
        fill(1, shift >> GRAIN.bit_length() - 1)
        fill(2, shift & (GRAIN - 1))
        for end in range(2):
            fill(3 + end, jnp.broadcast_to(range_ref[0, slot : slot + 1, end : end + 1], (1, 128)))
    floats[view] = jnp.broadcast_to(sharp_ref[...], (8, 128))
    pl.semaphore_wait(pltpu.get_barrier_semaphore(), expected)

    def window_copy(source, part, index, other, target_band):
        delta, begin, length, place = part
        return pltpu.make_async_remote_copy(
            src_ref=image_ref.at[pl.ds(begin, length)],
            dst_ref=window.at[source, pl.ds(place, length), pl.ds(PAD, cols)],
            send_sem=window_send.at[other, index],
            recv_sem=window_recv.at[source, index],
            **place_of(other, target_band, disp),
        )

    def own_copy(part, index):
        delta, begin, length, place = part
        return pltpu.make_async_copy(
            image_ref.at[pl.ds(begin, length)],
            window.at[view, pl.ds(place, length), pl.ds(PAD, cols)],
            window_recv.at[view, index],
        )

    def meta_copies(source, other):
        return [
            pltpu.make_async_remote_copy(
                src_ref=ref.at[source], dst_ref=ref.at[source],
                send_sem=meta_send.at[other, index], recv_sem=meta_recv.at[source, index],
                **place_of(other, band, disp),
            )
            for index, ref in enumerate((ints, floats))
        ]

    def sending(step, local):
        for other in range(views):

            @pl.when(view != other)
            def _():
                for copy in meta_copies(view, other):
                    step(copy)

            for row in rows_of[other]:
                aimed = row_of(other, disp, count) == row
                for index, part in enumerate(segments(row, count)):
                    if part[0] == 0:

                        @pl.when(aimed & (view != other))
                        def _():
                            step(window_copy(view, part, index, other, band))

                        if local:

                            @pl.when(aimed & (view == other))
                            def _():
                                own_copy(part, index).start()

                    else:

                        @pl.when(aimed & inside(band - part[0]))
                        def _():
                            step(window_copy(view, part, index, other, band - part[0]))

    sending(lambda copy: copy.start(), True)

    for other in range(views):

        @pl.when(view != other)
        def _():
            for copy in meta_copies(other, other):
                copy.wait_recv()

    table = pltpu.make_async_copy(ints, int_table, table_sem)
    table.start()

    def arrive(source):
        for row in range(count):
            for index, part in enumerate(segments(row, count)):
                if part[0] == 0:

                    @pl.when((mine == row) & (view != source))
                    def _():
                        window_copy(source, part, index, source, band).wait_recv()

                    @pl.when((mine == row) & (view == source))
                    def _():
                        own_copy(part, index).wait()

                else:

                    @pl.when((mine == row) & inside(band + part[0]))
                    def _():
                        window_copy(source, part, index, source, band + part[0]).wait_recv()

    for source in range(views):
        arrive(source)
        build(
            window.at[source], floats[source, 0:1, :] * math.log2(math.e),
            (left_cols.at[source], left_rows.at[source]) if source < views - 1 else None,
            (right_cols.at[source - 1], right_rows.at[source - 1]) if source > 0 else None,
        )
    table.wait()

    pairs = [(first, slot) for first in range(views - 1) for slot in range(min(slots, views - 1 - first))]

    def outcome(index, first, slot, side, place):
        target = first + side * (slot + 1)
        out = (left_ref, right_ref)[side].at[slot, pl.ds(mine, 1)]
        source = result.at[index, side]
        away = lambda: pltpu.make_async_remote_copy(
            src_ref=source, dst_ref=out,
            send_sem=result_send.at[index, side, place], recv_sem=result_recv.at[mine, side, slot],
            **place_of(target, band, place),
        )
        home = lambda: pltpu.make_async_copy(source, out, result_recv.at[mine, side, slot])
        return target, (away, home)

    def spread(index, first, slot, start):
        for side in range(2):
            for place in range(disps):
                target, (away, home) = outcome(index, first, slot, side, place)
                own = (target == view) & (disp == place)

                @pl.when(sends & jnp.logical_not(own))
                def _():
                    if start:
                        away().start()
                    else:
                        away().wait_send()

                if start:

                    @pl.when(sends & own)
                    def _():
                        home().start()

    def find(index):
        first = sum(jnp.where(index == at, pair[0], 0) for at, pair in enumerate(pairs))
        slot = sum(jnp.where(index == at, pair[1], 0) for at, pair in enumerate(pairs))
        return first, slot

    line = band * count + mine

    def match_pair(index, carry):
        first, slot = find(index)
        partner = first + slot + 1
        begin, end, pairing = (ints[first, pl.ds(kind * slots + slot, 1), :] for kind in (3, 4, 0))
        keep = jnp.where((begin <= line) & (end > line), pairing, 0).astype(jnp.float32)
        soft_pair(
            left_cols.at[first], left_rows.at[first], right_cols.at[partner - 1], right_rows.at[partner - 1],
            left_score, right_score, result.at[index, 0], result.at[index, 1],
            int_table[first, slots + slot, 0], int_table[first, 2 * slots + slot, 0], keep,
        )
        spread(index, first, slot, True)
        return carry

    lax.fori_loop(0, len(pairs), match_pair, 0)

    for row in range(count):
        own = member == row * share
        for side in range(2):
            for slot in range(slots):
                other = view + slot + 1 if side == 0 else view - slot - 1
                exists = (other >= 0) & (other < views)
                out = (left_ref, right_ref)[side].at[slot, pl.ds(row, 1)]
                source = result.at[0, side]

                @pl.when(exists & jnp.logical_not(own))
                def _():
                    pltpu.make_async_remote_copy(
                        src_ref=source, dst_ref=out,
                        send_sem=result_send.at[0, side, 0], recv_sem=result_recv.at[row, side, slot],
                        **place_of(row * share // disps, band, row * share % disps),
                    ).wait_recv()

                @pl.when(exists & own)
                def _():
                    pltpu.make_async_copy(source, out, result_recv.at[row, side, slot]).wait()

    sending(lambda copy: copy.wait_send(), False)
    for index, (first, slot) in enumerate(pairs):
        spread(index, first, slot, False)


def match(image, sharpness, paired, offset, row_range):
    views, disps = (lax.axis_size(axis) for axis in ("view", "disp"))
    count, cols = image.shape
    slots = paired.shape[1]
    pairs = sum(min(slots, views - 1 - first) for first in range(views - 1))
    entries = -(-5 * slots // 8) * 8
    hbm = pl.BlockSpec(memory_space=pl.ANY)
    vmem = pl.BlockSpec(memory_space=pltpu.VMEM)
    out = jax.ShapeDtypeStruct((slots, count, cols), jnp.float32)
    dma = pltpu.SemaphoreType.DMA
    return pl.pallas_call(
        functools.partial(match_kernel, slots),
        out_shape=(out, out),
        in_specs=[hbm] * 5,
        out_specs=(vmem, vmem),
        scratch_shapes=[
            pltpu.VMEM(sharpness.shape, jnp.float32),
            pltpu.VMEM(paired.shape, jnp.int32),
            pltpu.VMEM(offset.shape, jnp.int32),
            pltpu.VMEM(row_range.shape, jnp.int32),
            pltpu.VMEM((views, 16, cols + 2 * PAD), jnp.float32),
            pltpu.VMEM((views, entries, 128), jnp.int32),
            pltpu.VMEM((views, 8, 128), jnp.float32),
            pltpu.SMEM((views, entries, 128), jnp.int32),
            pltpu.VMEM((views - 1, DEPTH, cols), jnp.bfloat16),
            pltpu.VMEM((views - 1, cols + MARGIN, DEPTH), jnp.bfloat16),
            pltpu.VMEM((views - 1, DEPTH, cols), jnp.bfloat16),
            pltpu.VMEM((views - 1, cols + MARGIN, DEPTH), jnp.bfloat16),
            pltpu.VMEM((2, HALF, 128), jnp.float32),
            pltpu.VMEM((2, HALF, 128), jnp.float32),
            pltpu.VMEM((pairs, 2, 1, cols), jnp.float32),
            dma((views, 3)),
            dma((views, 3)),
            dma((views, 2)),
            dma((views, 2)),
            dma((4,)),
            dma,
            dma((pairs, 2, disps)),
            dma((count, 2, slots)),
        ],
        compiler_params=pltpu.CompilerParams(
            collective_id=0, has_side_effects=True, vmem_limit_bytes=40 * 1024 * 1024
        ),
        name="match",
    )(image, sharpness, paired, offset, row_range)


def shards(images, sharpness, paired, offset, row_range):
    left, right = match(images[0], sharpness[None], paired, offset, row_range)
    return (left[None], right[None])


def solution(mesh):
    return jax.shard_map(
        shards,
        mesh=mesh,
        in_specs=(
            P("view", "row", None),
            P("view"),
            P("view", None),
            P("view", None),
            P("view", None, None),
        ),
        out_specs=(P("view", None, "row", None), P("view", None, "row", None)),
        check_vma=False,
    )
```

```python
import functools
import math

import jax
import jax.numpy as jnp
from jax import lax
from jax.experimental import pallas as pl
from jax.experimental.pallas import tpu as pltpu
from jax.sharding import PartitionSpec as P

DISP = 256
RAD = 4
TAPS = 2 * RAD + 1
EPSILON = 1e-05
DEPTH = 256
PAD = 128
BLOCK = 256
GRAIN = 16
MARGIN = 384
SPAN = 2 * BLOCK
HALF = 3 * 128
EXTRA = DEPTH - GRAIN


def rounded(value):
    return value.astype(jnp.bfloat16).astype(jnp.float32)


def split3(value):
    high = rounded(value)
    middle = rounded(value - high)
    return (high, middle, value - high - middle)


def row_of(view, disp, row_count):
    group = lax.axis_size("view") * lax.axis_size("disp")
    return (view * lax.axis_size("disp") + disp) * row_count // group


def segments(row, row_count):
    found = []
    for delta in (-1, 0, 1):
        low = max(row - RAD, delta * row_count)
        high = min(row + RAD + 1, (delta + 1) * row_count)
        for begin, end in ((low, min(high, row + RAD)), (max(low, row + RAD), high)):
            if end > begin:
                found.append((delta, begin - delta * row_count, end - begin, begin - row + RAD))
    return found


def tiled(row, width):
    return jnp.concatenate([row] * (width // 128), axis=1)


def emit(values, end, order, mark, cols_ref):
    for index, value in enumerate(values):
        high = value.astype(jnp.bfloat16)
        parts = (high, (value - high.astype(jnp.float32)).astype(jnp.bfloat16))
        for group in range(3):
            start = (group * len(values) + index) * GRAIN
            cols_ref[start : start + GRAIN, :] = parts[order[group]]
    high = rounded(end)
    parts = (high, end - high)
    place = lax.broadcasted_iota(jnp.int32, (GRAIN, end.shape[1]), 0)
    rest = mark
    for group in range(3):
        rest = jnp.where(place == group, parts[order[group]], rest)
    cols_ref[EXTRA:DEPTH, :] = rest.astype(jnp.bfloat16)


def build(window_ref, gain, left_refs, right_refs):
    cols = window_ref.shape[1] - 2 * PAD
    sub = lax.broadcasted_iota(jnp.int32, (GRAIN, 128), 0)
    lane = lax.broadcasted_iota(jnp.int32, (GRAIN, DEPTH), 1) - EXTRA
    main = window_ref[0:8, :]
    last = window_ref[8:9, :]
    taps = [main[:, PAD - RAD + tap : PAD - RAD + tap + cols] for tap in range(TAPS)]
    fan = pltpu.roll(jnp.broadcast_to(last, main.shape), 0, 1, stride=1, stride_axis=0)
    taps.append(fan[:, PAD - RAD + 7 : PAD - RAD + 7 + cols])
    end = last[:, PAD + RAD : PAD + RAD + cols]
    values = [jnp.concatenate(taps[index : index + 2], axis=0) for index in range(0, TAPS + 1, 2)]
    total = values[0]
    for value in values[1:]:
        total = total + value
    mean = (jnp.sum(total, axis=0, keepdims=True) + end) * (1.0 / (TAPS * TAPS))
    values = [value - mean for value in values]
    end = end - mean
    total = values[0] * values[0]
    for value in values[1:]:
        total = total + value * value
    var = (jnp.sum(total, axis=0, keepdims=True) + end * end) * (1.0 / (TAPS * TAPS))
    scale = lax.rsqrt(var + EPSILON) * (1.0 / TAPS)
    zero = jnp.zeros((GRAIN, 128), jnp.float32)
    if right_refs is not None:
        cols_ref, rows_ref = right_refs
        mark = jnp.where((sub >= 6) & (sub < 9), 1.0, zero)
        emit([value * scale for value in values], end * scale, (0, 0, 1), tiled(mark, cols), cols_ref)
        rows_ref[MARGIN : MARGIN + cols, :] = cols_ref[...].T
        flag = jnp.where((lane >= 3) & (lane < 9), 1.0, 0.0).astype(jnp.bfloat16)
        rows_ref[0:MARGIN, :] = jnp.concatenate([flag] * (MARGIN // GRAIN), axis=0)
    if left_refs is not None:
        cols_ref, rows_ref = left_refs
        floor = [-part for part in split3(jnp.broadcast_to(gain, (GRAIN, 128)))]
        mark = zero
        for place in range(3):
            mark = jnp.where(sub == 3 + place, floor[place], mark)
        scale = scale * tiled(gain, cols)
        emit([value * scale for value in values], end * scale, (0, 1, 0), tiled(mark, cols), cols_ref)
        rows_ref[0:cols, :] = cols_ref[...].T
        edge = jnp.zeros((GRAIN, DEPTH), jnp.float32)
        for place in range(6):
            edge = jnp.where(lane == 3 + place, tiled(floor[place % 3], DEPTH), edge)
        rows_ref[cols : cols + MARGIN, :] = jnp.concatenate([edge.astype(jnp.bfloat16)] * (MARGIN // GRAIN), axis=0)


def turned(tiles, amount, forward):
    lane = lax.broadcasted_iota(jnp.int32, tiles[0].shape, 1)
    count = len(tiles)
    if forward:
        moved = [pltpu.roll(tile, amount, 1) for tile in tiles]
        return [jnp.where(lane < amount, moved[index - 1], moved[index]) for index in range(count)]
    moved = [pltpu.roll(tile, (128 - amount) & 127, 1) for tile in tiles]
    return [jnp.where(lane < 128 - amount, moved[index], moved[(index + 1) % count]) for index in range(count)]


class Turn:
    def __init__(self, source_ref, target_ref, amount, forward):
        self.source, self.target, self.forward = source_ref, target_ref, forward
        self.amount = amount if forward else (128 - amount) & 127
        self.edge = amount if forward else 128 - amount
        self.moved = {}

    def tile(self, index):
        if index not in self.moved:
            self.moved[index] = pltpu.roll(self.source[:, index * 128 : index * 128 + 128], self.amount, 1)
        return self.moved[index]

    def block(self, block):
        count = self.source.shape[1] // 128
        wide = BLOCK // 128
        for index in range(block * wide, block * wide + wide):
            lane = lax.broadcasted_iota(jnp.int32, (DEPTH, 128), 1)
            if self.forward:
                tile = jnp.where(lane < self.edge, self.tile(max(index - 1, 0)), self.tile(index))
            else:
                tile = jnp.where(lane < self.edge, self.tile(index), self.tile(min(index + 1, count - 1)))
            self.target[:, index * 128 : index * 128 + 128] = tile


def soft_half(score_ref, result_ref, column, left):
    lane = lax.broadcasted_iota(jnp.int32, (8, 128), 1)
    sub = lax.broadcasted_iota(jnp.int32, (8, 128), 0)
    skew = lane - sub
    sub_f = sub.astype(jnp.float32)
    lane_f = lane[0:1].astype(jnp.float32)
    slack = 0 if left else 1
    steps = DISP // 8
    corner = 128 // 8

    def load(step):
        return score_ref[8 * step : 8 * step + 8, :]

    near = [skew < 8 * step + slack for step in range(corner)]
    scores = [jnp.where(near[step], load(step), load(step + steps)) for step in range(corner)]
    scores += [load(step) for step in range(corner, steps)]
    tops = scores[:4]
    for step in range(4, steps):
        tops[step % 4] = jnp.maximum(tops[step % 4], scores[step])
    top = jnp.maximum(jnp.maximum(tops[0], tops[1]), jnp.maximum(tops[2], tops[3]))
    top = jnp.broadcast_to(jnp.max(top, axis=0, keepdims=True), (8, 128))
    zero = jnp.zeros((8, 128), jnp.float32)
    summed, running, far = ([zero, zero], [zero, zero], [zero, zero])
    for step in range(steps):
        weight = jnp.exp2(scores[step] - top)
        if step < corner:
            far[step % 2] = far[step % 2] + jnp.where(near[step], 0.0, weight)
        summed[step % 2] = summed[step % 2] + weight
        running[step % 2] = running[step % 2] + summed[step % 2]
    both = summed[0] + summed[1]
    moment = 8.0 * (steps * both - 2.0 * (running[0] + running[1]) + summed[1])
    moment = moment + sub_f * both + float(DISP) * (far[0] + far[1])
    total = jnp.sum(both, axis=0, keepdims=True)
    moment = jnp.sum(moment, axis=0, keepdims=True)
    if left:
        weighted = (lane_f + DISP) * total - moment
    else:
        weighted = moment - lane_f * total
    result_ref[:, column : column + 128] = weighted / (total * DISP)


def soft_pair(
    left_cols, left_rows, right_cols, right_rows, left_turned, right_turned, left_score, right_score, raw,
    left_result, right_result, coarse, fine, keep,
):
    cols = left_cols.shape[1]
    count = cols // BLOCK
    left_turn = Turn(left_cols, left_turned, fine, False)
    right_turn = Turn(right_cols, right_turned, fine, True)

    def scores(rows_ref, row_start, cols_ref, block, score_ref):
        score = jnp.dot(
            rows_ref[pl.ds(row_start * GRAIN, SPAN), :],
            cols_ref[:, block * BLOCK : (block + 1) * BLOCK],
            preferred_element_type=jnp.float32,
        )
        score_ref[0] = score[0:HALF, 0:128]
        score_ref[1] = score[128 : 128 + HALF, 128:256]

    def left_scores(block):
        scores(right_rows, block * (BLOCK // GRAIN) + (MARGIN - BLOCK) // GRAIN - coarse, left_turned, block, left_score)

    def right_scores(block):
        scores(left_rows, block * (BLOCK // GRAIN) + coarse, right_turned, block, right_score)

    def soft(score_ref, side, block, left):
        for half in range(2):
            soft_half(score_ref.at[half], raw.at[side], block * BLOCK + half * 128, left)

    left_turn.block(0)
    left_scores(0)
    right_turn.block(0)
    for block in range(count):
        right_scores(block)
        if block + 1 < count:
            left_turn.block(block + 1)
        soft(left_score, 0, block, True)
        if block + 1 < count:
            left_scores(block + 1)
            right_turn.block(block + 1)
        soft(right_score, 1, block, False)

    even = (DISP - 1) / (2.0 * DISP)
    lane = lax.broadcasted_iota(jnp.int32, (1, 128), 1)
    for side, result_ref in enumerate((left_result, right_result)):
        tiles = [jnp.broadcast_to(raw[side, :, start : start + 128], (8, 128)) for start in range(0, cols, 128)]
        tiles = [tile[0:1] for tile in turned(tiles, fine, side == 0)]
        if side == 0:
            tiles[0] = jnp.where(lane < fine, even, tiles[0])
        else:
            tiles[-1] = jnp.where(lane >= 128 - fine, even, tiles[-1])
        for index, tile in enumerate(tiles):
            result_ref[:, index * 128 : index * 128 + 128] = tile * keep


def place_of(view, row, disp):
    return dict(device_id={"view": view, "row": row, "disp": disp}, device_id_type=pl.DeviceIdType.MESH)


def signal(view, row, disp):
    pl.semaphore_signal(pltpu.get_barrier_semaphore(), inc=1, **place_of(view, row, disp))


def match_kernel(
    slots, image_ref, sharp_hbm, paired_hbm, offset_hbm, range_hbm, left_ref, right_ref,
    sharp_ref, paired_ref, offset_ref, range_ref, window, ints, floats, int_table,
    left_cols, left_rows, right_cols, right_rows, left_turned, right_turned, left_score, right_score, raw, result,
    window_send, window_recv, meta_send, meta_recv, scalar_sem, table_sem, result_send, result_recv,
):
    count, cols = image_ref.shape
    views, bands, disps = (lax.axis_size(axis) for axis in ("view", "row", "disp"))
    view, band, disp = (lax.axis_index(axis) for axis in ("view", "row", "disp"))
    group = views * disps
    share = group // count
    member = view * disps + disp
    mine = row_of(view, disp, count)
    sends = member % share == 0
    rows_of = [sorted({row_of(other, place, count) for place in range(disps)}) for other in range(views)]

    scalars = [
        pltpu.make_async_copy(source, target, scalar_sem.at[index])
        for index, (source, target) in enumerate(
            ((sharp_hbm, sharp_ref), (paired_hbm, paired_ref), (offset_hbm, offset_ref), (range_hbm, range_ref))
        )
    ]
    for copy in scalars:
        copy.start()
    window[...] = jnp.zeros_like(window)
    left_ref[...] = jnp.zeros_like(left_ref)
    right_ref[...] = jnp.zeros_like(right_ref)

    def inside(row):
        return (row >= 0) & (row < bands)

    for other in range(views):
        for place in range(disps):

            @pl.when((view != other) | (disp != place))
            def _():
                signal(other, band, place)

    expected = group - 1
    for delta in (-1, 1):
        needs = False
        wanted = 0
        for row in range(count):
            has = any(part[0] == delta for part in segments(row, count))
            needs = needs | ((mine == row) & has)
        for other in range(views):
            for row in rows_of[other]:
                if any(part[0] == delta for part in segments(row, count)):
                    wanted = wanted + jnp.where(row_of(other, disp, count) == row, 1, 0)

        @pl.when(needs & inside(band + delta))
        def _():
            for other in range(views):
                signal(other, band + delta, disp)

        expected = expected + jnp.where(inside(band - delta), wanted, 0)
    for copy in scalars:
        copy.wait()
    for slot in range(slots):

        def fill(kind, value):
            ints[view, kind * slots + slot : kind * slots + slot + 1] = value

        shift = jnp.broadcast_to(offset_ref[0:1, slot : slot + 1], (1, 128))
        fill(0, jnp.broadcast_to(paired_ref[0:1, slot : slot + 1], (1, 128)))
        fill(1, shift >> GRAIN.bit_length() - 1)
        fill(2, shift & (GRAIN - 1))
        for end in range(2):
            fill(3 + end, jnp.broadcast_to(range_ref[0, slot : slot + 1, end : end + 1], (1, 128)))
    floats[view] = jnp.broadcast_to(sharp_ref[...], (8, 128))
    pl.semaphore_wait(pltpu.get_barrier_semaphore(), expected)

    def window_copy(source, part, index, other, target_band):
        delta, begin, length, place = part
        return pltpu.make_async_remote_copy(
            src_ref=image_ref.at[pl.ds(begin, length)],
            dst_ref=window.at[source, pl.ds(place, length), pl.ds(PAD, cols)],
            send_sem=window_send.at[other, index],
            recv_sem=window_recv.at[source, index],
            **place_of(other, target_band, disp),
        )

    def own_copy(source, part, index):
        delta, begin, length, place = part
        return pltpu.make_async_copy(
            image_ref.at[pl.ds(begin, length)],
            window.at[source, pl.ds(place, length), pl.ds(PAD, cols)],
            window_recv.at[source, index],
        )

    def meta_copies(source, other):
        return [
            pltpu.make_async_remote_copy(
                src_ref=ref.at[source], dst_ref=ref.at[source],
                send_sem=meta_send.at[other, index], recv_sem=meta_recv.at[source, index],
                **place_of(other, band, disp),
            )
            for index, ref in enumerate((ints, floats))
        ]

    def sending(step, local):
        for other in range(views):

            @pl.when(view != other)
            def _():
                for copy in meta_copies(view, other):
                    step(copy)

            for row in rows_of[other]:

                @pl.when(row_of(other, disp, count) == row)
                def _():
                    for index, part in enumerate(segments(row, count)):
                        if part[0] != 0:

                            @pl.when(inside(band - part[0]))
                            def _():
                                step(window_copy(view, part, index, other, band - part[0]))

                    @pl.when(view != other)
                    def _():
                        for index, part in enumerate(segments(row, count)):
                            if part[0] == 0:
                                step(window_copy(view, part, index, other, band))

                    if local:

                        @pl.when(view == other)
                        def _():
                            for index, part in enumerate(segments(row, count)):
                                if part[0] == 0:
                                    own_copy(view, part, index).start()

    sending(lambda copy: copy.start(), True)

    for other in range(views):

        @pl.when(view != other)
        def _():
            for copy in meta_copies(other, other):
                copy.wait_recv()

    table = pltpu.make_async_copy(ints, int_table, table_sem)
    table.start()

    def arrive(source):
        for row in range(count):

            @pl.when(mine == row)
            def _():
                for index, part in enumerate(segments(row, count)):
                    if part[0] == 0:
                        own_copy(source, part, index).wait()
                    else:
                        pl.when(inside(band + part[0]))(own_copy(source, part, index).wait)

    for source in range(views):
        arrive(source)
        build(
            window.at[source], floats[source, 0:1, :] * math.log2(math.e),
            (left_cols.at[source], left_rows.at[source]) if source < views - 1 else None,
            (right_cols.at[source - 1], right_rows.at[source - 1]) if source > 0 else None,
        )
    table.wait()

    pairs = [(first, slot) for first in range(views - 1) for slot in range(min(slots, views - 1 - first))]

    def outcome(index, first, slot, side, place):
        target = first + side * (slot + 1)
        out = (left_ref, right_ref)[side].at[slot, pl.ds(mine, 1)]
        source = result.at[index, side]
        away = lambda: pltpu.make_async_remote_copy(
            src_ref=source, dst_ref=out,
            send_sem=result_send.at[index, side, place], recv_sem=result_recv.at[side, slot],
            **place_of(target, band, place),
        )
        home = lambda: pltpu.make_async_copy(source, out, result_recv.at[side, slot])
        return target, (away, home)

    def spread(index, first, slot, start):
        for side in range(2):
            for place in range(disps):
                target, (away, home) = outcome(index, first, slot, side, place)
                own = (target == view) & (disp == place)

                @pl.when(sends & jnp.logical_not(own))
                def _():
                    if start:
                        away().start()
                    else:
                        away().wait_send()

                if start:

                    @pl.when(sends & own)
                    def _():
                        home().start()

    def find(index):
        first = sum(jnp.where(index == at, pair[0], 0) for at, pair in enumerate(pairs))
        slot = sum(jnp.where(index == at, pair[1], 0) for at, pair in enumerate(pairs))
        return first, slot

    line = band * count + mine

    def match_pair(index, carry):
        first, slot = find(index)
        partner = first + slot + 1
        begin, end, pairing = (ints[first, pl.ds(kind * slots + slot, 1), :] for kind in (3, 4, 0))
        keep = jnp.where((begin <= line) & (end > line), pairing, 0).astype(jnp.float32)
        soft_pair(
            left_cols.at[first], left_rows.at[first], right_cols.at[partner - 1], right_rows.at[partner - 1],
            left_turned, right_turned, left_score, right_score, raw, result.at[index, 0], result.at[index, 1],
            int_table[first, slots + slot, 0], int_table[first, 2 * slots + slot, 0], keep,
        )
        spread(index, first, slot, True)
        return carry

    lax.fori_loop(0, len(pairs), match_pair, 0)

    sending(lambda copy: copy.wait_send(), False)
    for index, (first, slot) in enumerate(pairs):
        spread(index, first, slot, False)
    for side in range(2):
        for slot in range(slots):
            other = view + slot + 1 if side == 0 else view - slot - 1

            @pl.when((other >= 0) & (other < views))
            def _():
                out = (left_ref, right_ref)[side].at[slot]
                pltpu.make_async_copy(out, out, result_recv.at[side, slot]).wait()


def match(image, sharpness, paired, offset, row_range):
    views, disps = (lax.axis_size(axis) for axis in ("view", "disp"))
    count, cols = image.shape
    slots = paired.shape[1]
    pairs = sum(min(slots, views - 1 - first) for first in range(views - 1))
    entries = -(-5 * slots // 8) * 8
    hbm = pl.BlockSpec(memory_space=pl.ANY)
    vmem = pl.BlockSpec(memory_space=pltpu.VMEM)
    out = jax.ShapeDtypeStruct((slots, count, cols), jnp.float32)
    dma = pltpu.SemaphoreType.DMA
    return pl.pallas_call(
        functools.partial(match_kernel, slots),
        out_shape=(out, out),
        in_specs=[hbm] * 5,
        out_specs=(vmem, vmem),
        scratch_shapes=[
            pltpu.VMEM(sharpness.shape, jnp.float32),
            pltpu.VMEM(paired.shape, jnp.int32),
            pltpu.VMEM(offset.shape, jnp.int32),
            pltpu.VMEM(row_range.shape, jnp.int32),
            pltpu.VMEM((views, 16, cols + 2 * PAD), jnp.float32),
            pltpu.VMEM((views, entries, 128), jnp.int32),
            pltpu.VMEM((views, 8, 128), jnp.float32),
            pltpu.SMEM((views, entries, 128), jnp.int32),
            pltpu.VMEM((views - 1, DEPTH, cols), jnp.bfloat16),
            pltpu.VMEM((views - 1, cols + MARGIN, DEPTH), jnp.bfloat16),
            pltpu.VMEM((views - 1, DEPTH, cols), jnp.bfloat16),
            pltpu.VMEM((views - 1, cols + MARGIN, DEPTH), jnp.bfloat16),
            pltpu.VMEM((DEPTH, cols), jnp.bfloat16),
            pltpu.VMEM((DEPTH, cols), jnp.bfloat16),
            pltpu.VMEM((2, HALF, 128), jnp.float32),
            pltpu.VMEM((2, HALF, 128), jnp.float32),
            pltpu.VMEM((2, 1, cols), jnp.float32),
            pltpu.VMEM((pairs, 2, 1, cols), jnp.float32),
            dma((views, 3)),
            dma((views, 3)),
            dma((views, 2)),
            dma((views, 2)),
            dma((4,)),
            dma,
            dma((pairs, 2, disps)),
            dma((2, slots)),
        ],
        compiler_params=pltpu.CompilerParams(
            collective_id=0, has_side_effects=True, vmem_limit_bytes=40 * 1024 * 1024
        ),
        name="match",
    )(image, sharpness, paired, offset, row_range)


def settle_kernel(left_ref, right_ref, left_out, right_out, sems):
    copies = [
        pltpu.make_async_copy(source, target, sems.at[index])
        for index, (source, target) in enumerate(((left_ref, left_out), (right_ref, right_out)))
    ]
    for copy in copies:
        copy.start()
    for copy in copies:
        copy.wait()


def settle(left, right):
    anywhere = pl.BlockSpec(memory_space=pl.ANY)
    return pl.pallas_call(
        settle_kernel,
        out_shape=(left, right),
        in_specs=[pl.BlockSpec(memory_space=pltpu.VMEM)] * 2,
        out_specs=(anywhere, anywhere),
        scratch_shapes=[pltpu.SemaphoreType.DMA((2,))],
        compiler_params=pltpu.CompilerParams(vmem_limit_bytes=16 * 1024 * 1024),
        name="settle",
    )(left, right)


def shards(images, sharpness, paired, offset, row_range):
    left, right = match(images[0], sharpness[None], paired, offset, row_range)
    left, right = settle(left, right)
    return (left[None], right[None])


def solution(mesh):
    return jax.shard_map(
        shards,
        mesh=mesh,
        in_specs=(
            P("view", "row", None),
            P("view"),
            P("view", None),
            P("view", None),
            P("view", None, None),
        ),
        out_specs=(P("view", None, "row", None), P("view", None, "row", None)),
        check_vma=False,
    )
```

```python
import functools
import math

import jax
import jax.numpy as jnp
from jax import lax
from jax.experimental import pallas as pl
from jax.experimental.pallas import tpu as pltpu
from jax.sharding import PartitionSpec as P

DISP = 256
RAD = 4
TAPS = 2 * RAD + 1
EPSILON = 1e-05
DEPTH = 256
PAD = 128
BLOCK = 256
GRAIN = 16
MARGIN = 384
SPAN = 2 * BLOCK
HALF = 3 * 128
EXTRA = DEPTH - GRAIN


def rounded(value):
    return value.astype(jnp.bfloat16).astype(jnp.float32)


def split3(value):
    high = rounded(value)
    middle = rounded(value - high)
    return (high, middle, value - high - middle)


def row_of(view, disp, row_count):
    group = lax.axis_size("view") * lax.axis_size("disp")
    return (view * lax.axis_size("disp") + disp) * row_count // group


def segments(row, row_count):
    found = []
    for delta in (-1, 0, 1):
        low = max(row - RAD, delta * row_count)
        high = min(row + RAD + 1, (delta + 1) * row_count)
        for begin, end in ((low, min(high, row + RAD)), (max(low, row + RAD), high)):
            if end > begin:
                found.append((delta, begin - delta * row_count, end - begin, begin - row + RAD))
    return found


def tiled(row, width):
    return jnp.concatenate([row] * (width // 128), axis=1)


def emit(values, end, order, mark, cols_ref):
    for index, value in enumerate(values):
        high = value.astype(jnp.bfloat16)
        parts = (high, (value - high.astype(jnp.float32)).astype(jnp.bfloat16))
        for group in range(3):
            start = (group * len(values) + index) * GRAIN
            cols_ref[start : start + GRAIN, :] = parts[order[group]]
    high = rounded(end)
    parts = (high, end - high)
    place = lax.broadcasted_iota(jnp.int32, (GRAIN, end.shape[1]), 0)
    rest = mark
    for group in range(3):
        rest = jnp.where(place == group, parts[order[group]], rest)
    cols_ref[EXTRA:DEPTH, :] = rest.astype(jnp.bfloat16)


def build(window_ref, gain, left_refs, right_refs):
    cols = window_ref.shape[1] - 2 * PAD
    sub = lax.broadcasted_iota(jnp.int32, (GRAIN, 128), 0)
    lane = lax.broadcasted_iota(jnp.int32, (GRAIN, DEPTH), 1) - EXTRA
    main = window_ref[0:8, :]
    last = window_ref[8:9, :]
    taps = [main[:, PAD - RAD + tap : PAD - RAD + tap + cols] for tap in range(TAPS)]
    fan = pltpu.roll(jnp.broadcast_to(last, main.shape), 0, 1, stride=1, stride_axis=0)
    taps.append(fan[:, PAD - RAD + 7 : PAD - RAD + 7 + cols])
    end = last[:, PAD + RAD : PAD + RAD + cols]
    values = [jnp.concatenate(taps[index : index + 2], axis=0) for index in range(0, TAPS + 1, 2)]
    width = main.shape[1]
    sub8 = lax.broadcasted_iota(jnp.int32, main.shape, 0)
    sums = jnp.sum(main, axis=0, keepdims=True) + last
    squares = jnp.sum(main * main, axis=0, keepdims=True) + last * last
    total = jnp.where(sub8 < 4, sums, squares)
    double = total + pltpu.roll(total, width - 1, 1)
    double = double + pltpu.roll(double, width - 2, 1)
    double = double + pltpu.roll(double, width - 4, 1)
    total = double + pltpu.roll(total, width - 8, 1)
    total = total[:, PAD - RAD : PAD - RAD + cols] * (1.0 / (TAPS * TAPS))
    mean = total[0:1]
    var = total[4:5] - mean * mean
    values = [value - mean for value in values]
    end = end - mean
    scale = lax.rsqrt(var + EPSILON) * (1.0 / TAPS)
    zero = jnp.zeros((GRAIN, 128), jnp.float32)
    if right_refs is not None:
        cols_ref, rows_ref = right_refs
        mark = jnp.where((sub >= 6) & (sub < 9), 1.0, zero)
        emit([value * scale for value in values], end * scale, (0, 0, 1), tiled(mark, cols), cols_ref)
        rows_ref[MARGIN : MARGIN + cols, :] = cols_ref[...].T
        flag = jnp.where((lane >= 3) & (lane < 9), 1.0, 0.0).astype(jnp.bfloat16)
        rows_ref[0:MARGIN, :] = jnp.concatenate([flag] * (MARGIN // GRAIN), axis=0)
    if left_refs is not None:
        cols_ref, rows_ref = left_refs
        floor = [-part for part in split3(jnp.broadcast_to(gain, (GRAIN, 128)))]
        mark = zero
        for place in range(3):
            mark = jnp.where(sub == 3 + place, floor[place], mark)
        scale = scale * tiled(gain, cols)
        emit([value * scale for value in values], end * scale, (0, 1, 0), tiled(mark, cols), cols_ref)
        rows_ref[0:cols, :] = cols_ref[...].T
        edge = jnp.zeros((GRAIN, DEPTH), jnp.float32)
        for place in range(6):
            edge = jnp.where(lane == 3 + place, tiled(floor[place % 3], DEPTH), edge)
        rows_ref[cols : cols + MARGIN, :] = jnp.concatenate([edge.astype(jnp.bfloat16)] * (MARGIN // GRAIN), axis=0)


def turned(tiles, amount, forward):
    lane = lax.broadcasted_iota(jnp.int32, tiles[0].shape, 1)
    count = len(tiles)
    if forward:
        moved = [pltpu.roll(tile, amount, 1) for tile in tiles]
        return [jnp.where(lane < amount, moved[index - 1], moved[index]) for index in range(count)]
    moved = [pltpu.roll(tile, (128 - amount) & 127, 1) for tile in tiles]
    return [jnp.where(lane < 128 - amount, moved[index], moved[(index + 1) % count]) for index in range(count)]


class Turn:
    def __init__(self, source_ref, target_ref, amount, forward):
        self.source, self.target, self.forward = source_ref, target_ref, forward
        self.amount = amount if forward else (128 - amount) & 127
        self.edge = amount if forward else 128 - amount
        self.moved = {}
        size = EXTRA // 3
        self.parts = [(0, size), (2 * size, DEPTH)] if forward else [(0, 2 * size), (EXTRA, DEPTH)]
        self.copy = size if forward else 2 * size

    def tile(self, index, part):
        if (index, part) not in self.moved:
            begin, end = part
            self.moved[index, part] = pltpu.roll(self.source[begin:end, index * 128 : index * 128 + 128], self.amount, 1)
        return self.moved[index, part]

    def block(self, block):
        count = self.source.shape[1] // 128
        wide = BLOCK // 128
        size = EXTRA // 3
        for index in range(block * wide, block * wide + wide):
            place = slice(index * 128, index * 128 + 128)
            for part in self.parts:
                begin, end = part
                lane = lax.broadcasted_iota(jnp.int32, (end - begin, 128), 1)
                if self.forward:
                    tile = jnp.where(lane < self.edge, self.tile(max(index - 1, 0), part), self.tile(index, part))
                else:
                    tile = jnp.where(lane < self.edge, self.tile(index, part), self.tile(min(index + 1, count - 1), part))
                self.target[begin:end, place] = tile
                if begin == 0:
                    self.target[self.copy : self.copy + size, place] = tile[0:size]


def soft_half(score_ref, result_ref, column, left):
    lane = lax.broadcasted_iota(jnp.int32, (8, 128), 1)
    sub = lax.broadcasted_iota(jnp.int32, (8, 128), 0)
    skew = lane - sub
    sub_f = sub.astype(jnp.float32)
    lane_f = lane[0:1].astype(jnp.float32)
    slack = 0 if left else 1
    steps = DISP // 8
    corner = 128 // 8

    def load(step):
        return score_ref[8 * step : 8 * step + 8, :]

    near = [skew < 8 * step + slack for step in range(corner)]
    scores = [jnp.where(near[step], load(step), load(step + steps)) for step in range(corner)]
    scores += [load(step) for step in range(corner, steps)]
    tops = scores[:4]
    for step in range(4, steps):
        tops[step % 4] = jnp.maximum(tops[step % 4], scores[step])
    top = jnp.maximum(jnp.maximum(tops[0], tops[1]), jnp.maximum(tops[2], tops[3]))
    top = jnp.broadcast_to(jnp.max(top, axis=0, keepdims=True), (8, 128))
    zero = jnp.zeros((8, 128), jnp.float32)
    summed, running, far = ([zero, zero], [zero, zero], [zero, zero])
    for step in range(steps):
        weight = jnp.exp2(scores[step] - top)
        if step < corner:
            far[step % 2] = far[step % 2] + jnp.where(near[step], 0.0, weight)
        summed[step % 2] = summed[step % 2] + weight
        running[step % 2] = running[step % 2] + summed[step % 2]
    both = summed[0] + summed[1]
    moment = 8.0 * (steps * both - 2.0 * (running[0] + running[1]) + summed[1])
    moment = moment + sub_f * both + float(DISP) * (far[0] + far[1])
    total = jnp.sum(both, axis=0, keepdims=True)
    moment = jnp.sum(moment, axis=0, keepdims=True)
    if left:
        weighted = (lane_f + DISP) * total - moment
    else:
        weighted = moment - lane_f * total
    result_ref[:, column : column + 128] = weighted / (total * DISP)


def soft_pair(
    left_cols, left_rows, right_cols, right_rows, left_turned, right_turned, left_score, right_score, raw,
    left_result, right_result, coarse, fine, keep,
):
    cols = left_cols.shape[1]
    count = cols // BLOCK
    left_turn = Turn(left_cols, left_turned, fine, False)
    right_turn = Turn(right_cols, right_turned, fine, True)

    def scores(rows_ref, row_start, cols_ref, block, score_ref):
        score = jnp.dot(
            rows_ref[pl.ds(row_start * GRAIN, SPAN), :],
            cols_ref[:, block * BLOCK : (block + 1) * BLOCK],
            preferred_element_type=jnp.float32,
        )
        score_ref[0] = score[0:HALF, 0:128]
        score_ref[1] = score[128 : 128 + HALF, 128:256]

    def left_scores(block):
        scores(right_rows, block * (BLOCK // GRAIN) + (MARGIN - BLOCK) // GRAIN - coarse, left_turned, block, left_score)

    def right_scores(block):
        scores(left_rows, block * (BLOCK // GRAIN) + coarse, right_turned, block, right_score)

    def soft(score_ref, side, block, left):
        for half in range(2):
            soft_half(score_ref.at[half], raw.at[side], block * BLOCK + half * 128, left)

    left_turn.block(0)
    left_scores(0)
    right_turn.block(0)
    for block in range(count):
        right_scores(block)
        if block + 1 < count:
            left_turn.block(block + 1)
        soft(left_score, 0, block, True)
        if block + 1 < count:
            left_scores(block + 1)
            right_turn.block(block + 1)
        soft(right_score, 1, block, False)

    even = (DISP - 1) / (2.0 * DISP)
    lane = lax.broadcasted_iota(jnp.int32, (1, 128), 1)
    for side, result_ref in enumerate((left_result, right_result)):
        tiles = [jnp.broadcast_to(raw[side, :, start : start + 128], (8, 128)) for start in range(0, cols, 128)]
        tiles = [tile[0:1] for tile in turned(tiles, fine, side == 0)]
        if side == 0:
            tiles[0] = jnp.where(lane < fine, even, tiles[0])
        else:
            tiles[-1] = jnp.where(lane >= 128 - fine, even, tiles[-1])
        for index, tile in enumerate(tiles):
            result_ref[:, index * 128 : index * 128 + 128] = tile * keep


def place_of(view, row, disp):
    return dict(device_id={"view": view, "row": row, "disp": disp}, device_id_type=pl.DeviceIdType.MESH)


def signal(view, row, disp):
    pl.semaphore_signal(pltpu.get_barrier_semaphore(), inc=1, **place_of(view, row, disp))


def match_kernel(
    slots, image_ref, sharp_hbm, paired_hbm, offset_hbm, range_hbm, left_ref, right_ref,
    sharp_ref, paired_ref, offset_ref, range_ref, window, ints, floats, int_table,
    left_cols, left_rows, right_cols, right_rows, left_turned, right_turned, left_score, right_score, raw, result,
    window_send, window_recv, meta_send, meta_recv, scalar_sem, table_sem, result_send, result_recv,
):
    count, cols = image_ref.shape
    views, bands, disps = (lax.axis_size(axis) for axis in ("view", "row", "disp"))
    view, band, disp = (lax.axis_index(axis) for axis in ("view", "row", "disp"))
    group = views * disps
    share = group // count
    member = view * disps + disp
    mine = row_of(view, disp, count)
    sends = member % share == 0
    rows_of = [sorted({row_of(other, place, count) for place in range(disps)}) for other in range(views)]

    scalars = [
        pltpu.make_async_copy(source, target, scalar_sem.at[index])
        for index, (source, target) in enumerate(
            ((sharp_hbm, sharp_ref), (paired_hbm, paired_ref), (offset_hbm, offset_ref), (range_hbm, range_ref))
        )
    ]
    for copy in scalars:
        copy.start()
    window[...] = jnp.zeros_like(window)
    left_ref[...] = jnp.zeros_like(left_ref)
    right_ref[...] = jnp.zeros_like(right_ref)

    def inside(row):
        return (row >= 0) & (row < bands)

    for other in range(views):
        for place in range(disps):

            @pl.when((view != other) | (disp != place))
            def _():
                signal(other, band, place)

    expected = group - 1
    for delta in (-1, 1):
        needs = False
        wanted = 0
        for row in range(count):
            has = any(part[0] == delta for part in segments(row, count))
            needs = needs | ((mine == row) & has)
        for other in range(views):
            for row in rows_of[other]:
                if any(part[0] == delta for part in segments(row, count)):
                    wanted = wanted + jnp.where(row_of(other, disp, count) == row, 1, 0)

        @pl.when(needs & inside(band + delta))
        def _():
            for other in range(views):
                signal(other, band + delta, disp)

        expected = expected + jnp.where(inside(band - delta), wanted, 0)
    for copy in scalars:
        copy.wait()
    for slot in range(slots):

        def fill(kind, value):
            ints[view, kind * slots + slot : kind * slots + slot + 1] = value

        shift = jnp.broadcast_to(offset_ref[0:1, slot : slot + 1], (1, 128))
        fill(0, jnp.broadcast_to(paired_ref[0:1, slot : slot + 1], (1, 128)))
        fill(1, shift >> GRAIN.bit_length() - 1)
        fill(2, shift & (GRAIN - 1))
        for end in range(2):
            fill(3 + end, jnp.broadcast_to(range_ref[0, slot : slot + 1, end : end + 1], (1, 128)))
    floats[view] = jnp.broadcast_to(sharp_ref[...], (8, 128))
    pl.semaphore_wait(pltpu.get_barrier_semaphore(), expected)

    def window_copy(source, part, index, other, target_band):
        delta, begin, length, place = part
        return pltpu.make_async_remote_copy(
            src_ref=image_ref.at[pl.ds(begin, length)],
            dst_ref=window.at[source, pl.ds(place, length), pl.ds(PAD, cols)],
            send_sem=window_send.at[other, index],
            recv_sem=window_recv.at[source, index],
            **place_of(other, target_band, disp),
        )

    def own_copy(source, part, index):
        delta, begin, length, place = part
        return pltpu.make_async_copy(
            image_ref.at[pl.ds(begin, length)],
            window.at[source, pl.ds(place, length), pl.ds(PAD, cols)],
            window_recv.at[source, index],
        )

    def meta_copies(source, other):
        return [
            pltpu.make_async_remote_copy(
                src_ref=ref.at[source], dst_ref=ref.at[source],
                send_sem=meta_send.at[other, index], recv_sem=meta_recv.at[source, index],
                **place_of(other, band, disp),
            )
            for index, ref in enumerate((ints, floats))
        ]

    def sending(step, local):
        for other in range(views):

            @pl.when(view != other)
            def _():
                for copy in meta_copies(view, other):
                    step(copy)

            for row in rows_of[other]:

                @pl.when(row_of(other, disp, count) == row)
                def _():
                    for index, part in enumerate(segments(row, count)):
                        if part[0] != 0:

                            @pl.when(inside(band - part[0]))
                            def _():
                                step(window_copy(view, part, index, other, band - part[0]))

                    @pl.when(view != other)
                    def _():
                        for index, part in enumerate(segments(row, count)):
                            if part[0] == 0:
                                step(window_copy(view, part, index, other, band))

                    if local:

                        @pl.when(view == other)
                        def _():
                            for index, part in enumerate(segments(row, count)):
                                if part[0] == 0:
                                    own_copy(view, part, index).start()

    sending(lambda copy: copy.start(), True)

    for other in range(views):

        @pl.when(view != other)
        def _():
            for copy in meta_copies(other, other):
                copy.wait_recv()

    table = pltpu.make_async_copy(ints, int_table, table_sem)
    table.start()

    def arrive(source):
        for row in range(count):

            @pl.when(mine == row)
            def _():
                for index, part in enumerate(segments(row, count)):
                    if part[0] == 0:
                        own_copy(source, part, index).wait()
                    else:
                        pl.when(inside(band + part[0]))(own_copy(source, part, index).wait)

    for source in range(views):
        arrive(source)
        build(
            window.at[source], floats[source, 0:1, :] * math.log2(math.e),
            (left_cols.at[source], left_rows.at[source]) if source < views - 1 else None,
            (right_cols.at[source - 1], right_rows.at[source - 1]) if source > 0 else None,
        )
    table.wait()

    pairs = [(first, slot) for first in range(views - 1) for slot in range(min(slots, views - 1 - first))]

    def outcome(index, first, slot, side, place):
        target = first + side * (slot + 1)
        out = (left_ref, right_ref)[side].at[slot, pl.ds(mine, 1)]
        source = result.at[index, side]
        away = lambda: pltpu.make_async_remote_copy(
            src_ref=source, dst_ref=out,
            send_sem=result_send.at[index, side, place], recv_sem=result_recv.at[side, slot],
            **place_of(target, band, place),
        )
        home = lambda: pltpu.make_async_copy(source, out, result_recv.at[side, slot])
        return target, (away, home)

    def spread(index, first, slot, start):
        for side in range(2):
            for place in range(disps):
                target, (away, home) = outcome(index, first, slot, side, place)
                own = (target == view) & (disp == place)

                @pl.when(sends & jnp.logical_not(own))
                def _():
                    if start:
                        away().start()
                    else:
                        away().wait_send()

                if start:

                    @pl.when(sends & own)
                    def _():
                        home().start()

    def find(index):
        first = sum(jnp.where(index == at, pair[0], 0) for at, pair in enumerate(pairs))
        slot = sum(jnp.where(index == at, pair[1], 0) for at, pair in enumerate(pairs))
        return first, slot

    line = band * count + mine

    def match_pair(index, carry):
        first, slot = find(index)
        partner = first + slot + 1
        begin, end, pairing = (ints[first, pl.ds(kind * slots + slot, 1), :] for kind in (3, 4, 0))
        keep = jnp.where((begin <= line) & (end > line), pairing, 0).astype(jnp.float32)
        soft_pair(
            left_cols.at[first], left_rows.at[first], right_cols.at[partner - 1], right_rows.at[partner - 1],
            left_turned, right_turned, left_score, right_score, raw, result.at[index, 0], result.at[index, 1],
            int_table[first, slots + slot, 0], int_table[first, 2 * slots + slot, 0], keep,
        )
        spread(index, first, slot, True)
        return carry

    lax.fori_loop(0, len(pairs), match_pair, 0)

    sending(lambda copy: copy.wait_send(), False)
    for index, (first, slot) in enumerate(pairs):
        spread(index, first, slot, False)
    for side in range(2):
        for slot in range(slots):
            other = view + slot + 1 if side == 0 else view - slot - 1

            @pl.when((other >= 0) & (other < views))
            def _():
                out = (left_ref, right_ref)[side].at[slot]
                pltpu.make_async_copy(out, out, result_recv.at[side, slot]).wait()


def match(image, sharpness, paired, offset, row_range):
    views, disps = (lax.axis_size(axis) for axis in ("view", "disp"))
    count, cols = image.shape
    slots = paired.shape[1]
    pairs = sum(min(slots, views - 1 - first) for first in range(views - 1))
    entries = -(-5 * slots // 8) * 8
    hbm = pl.BlockSpec(memory_space=pl.ANY)
    vmem = pl.BlockSpec(memory_space=pltpu.VMEM)
    out = jax.ShapeDtypeStruct((slots, count, cols), jnp.float32)
    dma = pltpu.SemaphoreType.DMA
    return pl.pallas_call(
        functools.partial(match_kernel, slots),
        out_shape=(out, out),
        in_specs=[hbm] * 5,
        out_specs=(vmem, vmem),
        scratch_shapes=[
            pltpu.VMEM(sharpness.shape, jnp.float32),
            pltpu.VMEM(paired.shape, jnp.int32),
            pltpu.VMEM(offset.shape, jnp.int32),
            pltpu.VMEM(row_range.shape, jnp.int32),
            pltpu.VMEM((views, 16, cols + 2 * PAD), jnp.float32),
            pltpu.VMEM((views, entries, 128), jnp.int32),
            pltpu.VMEM((views, 8, 128), jnp.float32),
            pltpu.SMEM((views, entries, 128), jnp.int32),
            pltpu.VMEM((views - 1, DEPTH, cols), jnp.bfloat16),
            pltpu.VMEM((views - 1, cols + MARGIN, DEPTH), jnp.bfloat16),
            pltpu.VMEM((views - 1, DEPTH, cols), jnp.bfloat16),
            pltpu.VMEM((views - 1, cols + MARGIN, DEPTH), jnp.bfloat16),
            pltpu.VMEM((DEPTH, cols), jnp.bfloat16),
            pltpu.VMEM((DEPTH, cols), jnp.bfloat16),
            pltpu.VMEM((2, HALF, 128), jnp.float32),
            pltpu.VMEM((2, HALF, 128), jnp.float32),
            pltpu.VMEM((2, 1, cols), jnp.float32),
            pltpu.VMEM((pairs, 2, 1, cols), jnp.float32),
            dma((views, 3)),
            dma((views, 3)),
            dma((views, 2)),
            dma((views, 2)),
            dma((4,)),
            dma,
            dma((pairs, 2, disps)),
            dma((2, slots)),
        ],
        compiler_params=pltpu.CompilerParams(
            collective_id=0, has_side_effects=True, vmem_limit_bytes=40 * 1024 * 1024
        ),
        name="match",
    )(image, sharpness, paired, offset, row_range)


def settle_kernel(left_ref, right_ref, left_out, right_out, sems):
    copies = [
        pltpu.make_async_copy(source, target, sems.at[index])
        for index, (source, target) in enumerate(((left_ref, left_out), (right_ref, right_out)))
    ]
    for copy in copies:
        copy.start()
    for copy in copies:
        copy.wait()


def settle(left, right):
    anywhere = pl.BlockSpec(memory_space=pl.ANY)
    return pl.pallas_call(
        settle_kernel,
        out_shape=(left, right),
        in_specs=[pl.BlockSpec(memory_space=pltpu.VMEM)] * 2,
        out_specs=(anywhere, anywhere),
        scratch_shapes=[pltpu.SemaphoreType.DMA((2,))],
        compiler_params=pltpu.CompilerParams(vmem_limit_bytes=16 * 1024 * 1024),
        name="settle",
    )(left, right)


def shards(images, sharpness, paired, offset, row_range):
    left, right = match(images[0], sharpness[None], paired, offset, row_range)
    left, right = settle(left, right)
    return (left[None], right[None])


def solution(mesh):
    return jax.shard_map(
        shards,
        mesh=mesh,
        in_specs=(
            P("view", "row", None),
            P("view"),
            P("view", None),
            P("view", None),
            P("view", None, None),
        ),
        out_specs=(P("view", None, "row", None), P("view", None, "row", None)),
        check_vma=False,
    )
```

```python
import functools
import math

import jax
import jax.numpy as jnp
from jax import lax
from jax.experimental import pallas as pl
from jax.experimental.pallas import tpu as pltpu
from jax.sharding import PartitionSpec as P

DISP = 256
RAD = 4
TAPS = 2 * RAD + 1
EPSILON = 1e-05
DEPTH = 256
PAD = 128
BLOCK = 256
GRAIN = 16
MARGIN = 384
SPAN = 2 * BLOCK
HALF = 3 * 128
EXTRA = DEPTH - GRAIN


def rounded(value):
    return value.astype(jnp.bfloat16).astype(jnp.float32)


def split3(value):
    high = rounded(value)
    middle = rounded(value - high)
    return (high, middle, value - high - middle)


def row_of(view, disp, row_count):
    group = lax.axis_size("view") * lax.axis_size("disp")
    return (view * lax.axis_size("disp") + disp) * row_count // group


def segments(row, row_count):
    found = []
    for delta in (-1, 0, 1):
        low = max(row - RAD, delta * row_count)
        high = min(row + RAD + 1, (delta + 1) * row_count)
        for begin, end in ((low, min(high, row + RAD)), (max(low, row + RAD), high)):
            if end > begin:
                found.append((delta, begin - delta * row_count, end - begin, begin - row + RAD))
    return found


def tiled(row, width):
    return jnp.concatenate([row] * (width // 128), axis=1)


def emit(values, end, order, mark, cols_ref):
    for index, value in enumerate(values):
        high = value.astype(jnp.bfloat16)
        parts = (high, (value - high.astype(jnp.float32)).astype(jnp.bfloat16))
        for group in range(3):
            start = (group * len(values) + index) * GRAIN
            cols_ref[start : start + GRAIN, :] = parts[order[group]]
    high = rounded(end)
    parts = (high, end - high)
    place = lax.broadcasted_iota(jnp.int32, (GRAIN, end.shape[1]), 0)
    rest = mark
    for group in range(3):
        rest = jnp.where(place == group, parts[order[group]], rest)
    cols_ref[EXTRA:DEPTH, :] = rest.astype(jnp.bfloat16)


def build(window_ref, gain, left_refs, right_refs):
    cols = window_ref.shape[1] - 2 * PAD
    sub = lax.broadcasted_iota(jnp.int32, (GRAIN, 128), 0)
    lane = lax.broadcasted_iota(jnp.int32, (GRAIN, DEPTH), 1) - EXTRA
    main = window_ref[0:8, :]
    last = window_ref[8:9, :]
    taps = [main[:, PAD - RAD + tap : PAD - RAD + tap + cols] for tap in range(TAPS)]
    fan = pltpu.roll(jnp.broadcast_to(last, main.shape), 0, 1, stride=1, stride_axis=0)
    taps.append(fan[:, PAD - RAD + 7 : PAD - RAD + 7 + cols])
    end = last[:, PAD + RAD : PAD + RAD + cols]
    values = [jnp.concatenate(taps[index : index + 2], axis=0) for index in range(0, TAPS + 1, 2)]
    width = main.shape[1]
    sub8 = lax.broadcasted_iota(jnp.int32, main.shape, 0)
    sums = jnp.sum(main, axis=0, keepdims=True) + last
    squares = jnp.sum(main * main, axis=0, keepdims=True) + last * last
    total = jnp.where(sub8 < 4, sums, squares)
    double = total + pltpu.roll(total, width - 1, 1)
    double = double + pltpu.roll(double, width - 2, 1)
    double = double + pltpu.roll(double, width - 4, 1)
    total = double + pltpu.roll(total, width - 8, 1)
    total = total[:, PAD - RAD : PAD - RAD + cols] * (1.0 / (TAPS * TAPS))
    mean = total[0:1]
    var = total[4:5] - mean * mean
    values = [value - mean for value in values]
    end = end - mean
    scale = lax.rsqrt(var + EPSILON) * (1.0 / TAPS)
    zero = jnp.zeros((GRAIN, 128), jnp.float32)
    if right_refs is not None:
        cols_ref, rows_ref = right_refs
        mark = jnp.where((sub >= 6) & (sub < 9), 1.0, zero)
        emit([value * scale for value in values], end * scale, (0, 0, 1), tiled(mark, cols), cols_ref)
        rows_ref[MARGIN : MARGIN + cols, :] = cols_ref[...].T
        flag = jnp.where((lane >= 3) & (lane < 9), 1.0, 0.0).astype(jnp.bfloat16)
        rows_ref[0:MARGIN, :] = jnp.concatenate([flag] * (MARGIN // GRAIN), axis=0)
    if left_refs is not None:
        cols_ref, rows_ref = left_refs
        floor = [-part for part in split3(jnp.broadcast_to(gain, (GRAIN, 128)))]
        mark = zero
        for place in range(3):
            mark = jnp.where(sub == 3 + place, floor[place], mark)
        scale = scale * tiled(gain, cols)
        emit([value * scale for value in values], end * scale, (0, 1, 0), tiled(mark, cols), cols_ref)
        rows_ref[0:cols, :] = cols_ref[...].T
        edge = jnp.zeros((GRAIN, DEPTH), jnp.float32)
        for place in range(6):
            edge = jnp.where(lane == 3 + place, tiled(floor[place % 3], DEPTH), edge)
        rows_ref[cols : cols + MARGIN, :] = jnp.concatenate([edge.astype(jnp.bfloat16)] * (MARGIN // GRAIN), axis=0)


def turned(tiles, amount, forward):
    lane = lax.broadcasted_iota(jnp.int32, tiles[0].shape, 1)
    count = len(tiles)
    if forward:
        moved = [pltpu.roll(tile, amount, 1) for tile in tiles]
        return [jnp.where(lane < amount, moved[index - 1], moved[index]) for index in range(count)]
    moved = [pltpu.roll(tile, (128 - amount) & 127, 1) for tile in tiles]
    return [jnp.where(lane < 128 - amount, moved[index], moved[(index + 1) % count]) for index in range(count)]


class Turn:
    def __init__(self, source_ref, target_ref, amount, forward):
        self.source, self.target, self.forward = source_ref, target_ref, forward
        self.amount = amount if forward else (128 - amount) & 127
        self.edge = amount if forward else 128 - amount
        self.moved = {}
        size = EXTRA // 3
        self.parts = [(0, size), (2 * size, DEPTH)] if forward else [(0, 2 * size), (EXTRA, DEPTH)]
        self.copy = size if forward else 2 * size

    def tile(self, index, part):
        if (index, part) not in self.moved:
            begin, end = part
            self.moved[index, part] = pltpu.roll(self.source[begin:end, index * 128 : index * 128 + 128], self.amount, 1)
        return self.moved[index, part]

    def block(self, block):
        count = self.source.shape[1] // 128
        wide = BLOCK // 128
        size = EXTRA // 3
        for index in range(block * wide, block * wide + wide):
            place = slice(index * 128, index * 128 + 128)
            for part in self.parts:
                begin, end = part
                lane = lax.broadcasted_iota(jnp.int32, (end - begin, 128), 1)
                if self.forward:
                    tile = jnp.where(lane < self.edge, self.tile(max(index - 1, 0), part), self.tile(index, part))
                else:
                    tile = jnp.where(lane < self.edge, self.tile(index, part), self.tile(min(index + 1, count - 1), part))
                self.target[begin:end, place] = tile
                if begin == 0:
                    self.target[self.copy : self.copy + size, place] = tile[0:size]


def soft_half(score_ref, result_ref, column, left):
    lane = lax.broadcasted_iota(jnp.int32, (8, 128), 1)
    sub = lax.broadcasted_iota(jnp.int32, (8, 128), 0)
    skew = lane - sub
    sub_f = sub.astype(jnp.float32)
    lane_f = lane[0:1].astype(jnp.float32)
    slack = 0 if left else 1
    steps = DISP // 8
    corner = 128 // 8

    def load(step):
        return score_ref[8 * step : 8 * step + 8, :]

    near = [skew < 8 * step + slack for step in range(corner)]
    scores = [jnp.where(near[step], load(step), load(step + steps)) for step in range(corner)]
    scores += [load(step) for step in range(corner, steps)]
    tops = scores[:4]
    for step in range(4, steps):
        tops[step % 4] = jnp.maximum(tops[step % 4], scores[step])
    top = jnp.maximum(jnp.maximum(tops[0], tops[1]), jnp.maximum(tops[2], tops[3]))
    top = jnp.broadcast_to(jnp.max(top, axis=0, keepdims=True), (8, 128))
    zero = jnp.zeros((8, 128), jnp.float32)
    summed, running, far = ([zero, zero], [zero, zero], [zero, zero])
    for step in range(steps):
        weight = jnp.exp2(scores[step] - top)
        if step < corner:
            far[step % 2] = far[step % 2] + jnp.where(near[step], 0.0, weight)
        summed[step % 2] = summed[step % 2] + weight
        running[step % 2] = running[step % 2] + summed[step % 2]
    both = summed[0] + summed[1]
    moment = 8.0 * (steps * both - 2.0 * (running[0] + running[1]) + summed[1])
    moment = moment + sub_f * both + float(DISP) * (far[0] + far[1])
    total = jnp.sum(both, axis=0, keepdims=True)
    moment = jnp.sum(moment, axis=0, keepdims=True)
    if left:
        weighted = (lane_f + DISP) * total - moment
    else:
        weighted = moment - lane_f * total
    result_ref[:, column : column + 128] = weighted / (total * DISP)


def soft_pair(
    left_cols, left_rows, right_cols, right_rows, left_turned, right_turned, left_score, right_score, raw,
    left_result, right_result, coarse, fine, keep,
):
    cols = left_cols.shape[1]
    count = cols // BLOCK
    left_turn = Turn(left_cols, left_turned, fine, False)
    right_turn = Turn(right_cols, right_turned, fine, True)

    def scores(rows_ref, row_start, cols_ref, block, score_ref):
        score = jnp.dot(
            rows_ref[pl.ds(row_start * GRAIN, SPAN), :],
            cols_ref[:, block * BLOCK : (block + 1) * BLOCK],
            preferred_element_type=jnp.float32,
        )
        score_ref[0] = score[0:HALF, 0:128]
        score_ref[1] = score[128 : 128 + HALF, 128:256]

    def left_scores(block):
        scores(right_rows, block * (BLOCK // GRAIN) + (MARGIN - BLOCK) // GRAIN - coarse, left_turned, block, left_score)

    def right_scores(block):
        scores(left_rows, block * (BLOCK // GRAIN) + coarse, right_turned, block, right_score)

    def soft(score_ref, side, block, left):
        for half in range(2):
            soft_half(score_ref.at[half], raw.at[side], block * BLOCK + half * 128, left)

    left_turn.block(0)
    left_scores(0)
    right_turn.block(0)
    for block in range(count):
        right_scores(block)
        if block + 1 < count:
            left_turn.block(block + 1)
        soft(left_score, 0, block, True)
        if block + 1 < count:
            left_scores(block + 1)
            right_turn.block(block + 1)
        soft(right_score, 1, block, False)

    even = (DISP - 1) / (2.0 * DISP)
    lane = lax.broadcasted_iota(jnp.int32, (1, 128), 1)
    for side, result_ref in enumerate((left_result, right_result)):
        tiles = [jnp.broadcast_to(raw[side, :, start : start + 128], (8, 128)) for start in range(0, cols, 128)]
        tiles = [tile[0:1] for tile in turned(tiles, fine, side == 0)]
        if side == 0:
            tiles[0] = jnp.where(lane < fine, even, tiles[0])
        else:
            tiles[-1] = jnp.where(lane >= 128 - fine, even, tiles[-1])
        for index, tile in enumerate(tiles):
            result_ref[:, index * 128 : index * 128 + 128] = tile * keep


def place_of(view, row, disp):
    return dict(device_id={"view": view, "row": row, "disp": disp}, device_id_type=pl.DeviceIdType.MESH)


def signal(view, row, disp):
    pl.semaphore_signal(pltpu.get_barrier_semaphore(), inc=1, **place_of(view, row, disp))


def match_kernel(
    slots, image_ref, sharp_hbm, paired_hbm, offset_hbm, range_hbm, left_ref, right_ref,
    sharp_ref, paired_ref, offset_ref, range_ref, window, ints, floats, int_table,
    left_cols, left_rows, right_cols, right_rows, left_turned, right_turned, left_score, right_score, raw, result, empty,
    window_send, window_recv, meta_send, meta_recv, scalar_sem, table_sem, result_send, result_recv,
):
    count, cols = image_ref.shape
    views, bands, disps = (lax.axis_size(axis) for axis in ("view", "row", "disp"))
    view, band, disp = (lax.axis_index(axis) for axis in ("view", "row", "disp"))
    group = views * disps
    share = group // count
    member = view * disps + disp
    mine = row_of(view, disp, count)
    sends = member % share == 0
    rows_of = [sorted({row_of(other, place, count) for place in range(disps)}) for other in range(views)]

    scalars = [
        pltpu.make_async_copy(source, target, scalar_sem.at[index])
        for index, (source, target) in enumerate(
            ((sharp_hbm, sharp_ref), (paired_hbm, paired_ref), (offset_hbm, offset_ref), (range_hbm, range_ref))
        )
    ]
    for copy in scalars:
        copy.start()
    window[...] = jnp.zeros_like(window)
    empty[...] = jnp.zeros_like(empty)

    def clearing(step):
        for side in range(2):
            for slot in range(slots):
                other = view + slot + 1 if side == 0 else view - slot - 1

                @pl.when((other < 0) | (other >= views))
                def _():
                    step(pltpu.make_async_copy(empty, (left_ref, right_ref)[side].at[slot], result_recv.at[side, slot]))

    clearing(lambda copy: copy.start())

    def inside(row):
        return (row >= 0) & (row < bands)

    for other in range(views):
        for place in range(disps):

            @pl.when((view != other) | (disp != place))
            def _():
                signal(other, band, place)

    expected = group - 1
    for delta in (-1, 1):
        needs = False
        wanted = 0
        for row in range(count):
            has = any(part[0] == delta for part in segments(row, count))
            needs = needs | ((mine == row) & has)
        for other in range(views):
            for row in rows_of[other]:
                if any(part[0] == delta for part in segments(row, count)):
                    wanted = wanted + jnp.where(row_of(other, disp, count) == row, 1, 0)

        @pl.when(needs & inside(band + delta))
        def _():
            for other in range(views):
                signal(other, band + delta, disp)

        expected = expected + jnp.where(inside(band - delta), wanted, 0)
    for copy in scalars:
        copy.wait()
    for slot in range(slots):

        def fill(kind, value):
            ints[view, kind * slots + slot : kind * slots + slot + 1] = value

        shift = jnp.broadcast_to(offset_ref[0:1, slot : slot + 1], (1, 128))
        fill(0, jnp.broadcast_to(paired_ref[0:1, slot : slot + 1], (1, 128)))
        fill(1, shift >> GRAIN.bit_length() - 1)
        fill(2, shift & (GRAIN - 1))
        for end in range(2):
            fill(3 + end, jnp.broadcast_to(range_ref[0, slot : slot + 1, end : end + 1], (1, 128)))
    floats[view] = jnp.broadcast_to(sharp_ref[...], (8, 128))
    pl.semaphore_wait(pltpu.get_barrier_semaphore(), expected)

    def window_copy(source, part, index, other, target_band):
        delta, begin, length, place = part
        return pltpu.make_async_remote_copy(
            src_ref=image_ref.at[pl.ds(begin, length)],
            dst_ref=window.at[source, pl.ds(place, length), pl.ds(PAD, cols)],
            send_sem=window_send.at[other, index],
            recv_sem=window_recv.at[source, index],
            **place_of(other, target_band, disp),
        )

    def own_copy(source, part, index):
        delta, begin, length, place = part
        return pltpu.make_async_copy(
            image_ref.at[pl.ds(begin, length)],
            window.at[source, pl.ds(place, length), pl.ds(PAD, cols)],
            window_recv.at[source, index],
        )

    def meta_copies(source, other):
        return [
            pltpu.make_async_remote_copy(
                src_ref=ref.at[source], dst_ref=ref.at[source],
                send_sem=meta_send.at[other, index], recv_sem=meta_recv.at[source, index],
                **place_of(other, band, disp),
            )
            for index, ref in enumerate((ints, floats))
        ]

    def sending(step, local):
        for other in range(views):

            @pl.when(view != other)
            def _():
                for copy in meta_copies(view, other):
                    step(copy)

            for row in rows_of[other]:

                @pl.when(row_of(other, disp, count) == row)
                def _():
                    for index, part in enumerate(segments(row, count)):
                        if part[0] != 0:

                            @pl.when(inside(band - part[0]))
                            def _():
                                step(window_copy(view, part, index, other, band - part[0]))

                    @pl.when(view != other)
                    def _():
                        for index, part in enumerate(segments(row, count)):
                            if part[0] == 0:
                                step(window_copy(view, part, index, other, band))

                    if local:

                        @pl.when(view == other)
                        def _():
                            for index, part in enumerate(segments(row, count)):
                                if part[0] == 0:
                                    own_copy(view, part, index).start()

    sending(lambda copy: copy.start(), True)

    for other in range(views):

        @pl.when(view != other)
        def _():
            for copy in meta_copies(other, other):
                copy.wait_recv()

    table = pltpu.make_async_copy(ints, int_table, table_sem)
    table.start()

    def arrive(source):
        for row in range(count):

            @pl.when(mine == row)
            def _():
                for index, part in enumerate(segments(row, count)):
                    if part[0] == 0:
                        own_copy(source, part, index).wait()
                    else:
                        pl.when(inside(band + part[0]))(own_copy(source, part, index).wait)

    for source in range(views):
        arrive(source)
        build(
            window.at[source], floats[source, 0:1, :] * math.log2(math.e),
            (left_cols.at[source], left_rows.at[source]) if source < views - 1 else None,
            (right_cols.at[source - 1], right_rows.at[source - 1]) if source > 0 else None,
        )
    table.wait()

    pairs = [(first, slot) for first in range(views - 1) for slot in range(min(slots, views - 1 - first))]

    def outcome(index, first, slot, side, place):
        target = first + side * (slot + 1)
        out = (left_ref, right_ref)[side].at[slot, pl.ds(mine, 1)]
        source = result.at[index, side]
        away = lambda: pltpu.make_async_remote_copy(
            src_ref=source, dst_ref=out,
            send_sem=result_send.at[index, side, place], recv_sem=result_recv.at[side, slot],
            **place_of(target, band, place),
        )
        home = lambda: pltpu.make_async_copy(source, out, result_recv.at[side, slot])
        return target, (away, home)

    def spread(index, first, slot, start):
        for side in range(2):
            for place in range(disps):
                target, (away, home) = outcome(index, first, slot, side, place)
                own = (target == view) & (disp == place)

                @pl.when(sends & jnp.logical_not(own))
                def _():
                    if start:
                        away().start()
                    else:
                        away().wait_send()

                if start:

                    @pl.when(sends & own)
                    def _():
                        home().start()

    def find(index):
        first = sum(jnp.where(index == at, pair[0], 0) for at, pair in enumerate(pairs))
        slot = sum(jnp.where(index == at, pair[1], 0) for at, pair in enumerate(pairs))
        return first, slot

    line = band * count + mine

    def match_pair(index, carry):
        first, slot = find(index)
        partner = first + slot + 1
        begin, end, pairing = (ints[first, pl.ds(kind * slots + slot, 1), :] for kind in (3, 4, 0))
        keep = jnp.where((begin <= line) & (end > line), pairing, 0).astype(jnp.float32)
        soft_pair(
            left_cols.at[first], left_rows.at[first], right_cols.at[partner - 1], right_rows.at[partner - 1],
            left_turned, right_turned, left_score, right_score, raw, result.at[index, 0], result.at[index, 1],
            int_table[first, slots + slot, 0], int_table[first, 2 * slots + slot, 0], keep,
        )
        spread(index, first, slot, True)
        return carry

    lax.fori_loop(0, len(pairs), match_pair, 0)

    sending(lambda copy: copy.wait_send(), False)
    for index, (first, slot) in enumerate(pairs):
        spread(index, first, slot, False)
    clearing(lambda copy: copy.wait())
    for side in range(2):
        for slot in range(slots):
            other = view + slot + 1 if side == 0 else view - slot - 1

            @pl.when((other >= 0) & (other < views))
            def _():
                out = (left_ref, right_ref)[side].at[slot]
                pltpu.make_async_copy(out, out, result_recv.at[side, slot]).wait()


def match(image, sharpness, paired, offset, row_range):
    views, disps = (lax.axis_size(axis) for axis in ("view", "disp"))
    count, cols = image.shape
    slots = paired.shape[1]
    pairs = sum(min(slots, views - 1 - first) for first in range(views - 1))
    entries = -(-5 * slots // 8) * 8
    anywhere = pl.BlockSpec(memory_space=pl.ANY)
    out = jax.ShapeDtypeStruct((slots, count, cols), jnp.float32)
    dma = pltpu.SemaphoreType.DMA
    return pl.pallas_call(
        functools.partial(match_kernel, slots),
        out_shape=(out, out),
        in_specs=[anywhere] * 5,
        out_specs=(anywhere, anywhere),
        scratch_shapes=[
            pltpu.VMEM(sharpness.shape, jnp.float32),
            pltpu.VMEM(paired.shape, jnp.int32),
            pltpu.VMEM(offset.shape, jnp.int32),
            pltpu.VMEM(row_range.shape, jnp.int32),
            pltpu.VMEM((views, 16, cols + 2 * PAD), jnp.float32),
            pltpu.VMEM((views, entries, 128), jnp.int32),
            pltpu.VMEM((views, 8, 128), jnp.float32),
            pltpu.SMEM((views, entries, 128), jnp.int32),
            pltpu.VMEM((views - 1, DEPTH, cols), jnp.bfloat16),
            pltpu.VMEM((views - 1, cols + MARGIN, DEPTH), jnp.bfloat16),
            pltpu.VMEM((views - 1, DEPTH, cols), jnp.bfloat16),
            pltpu.VMEM((views - 1, cols + MARGIN, DEPTH), jnp.bfloat16),
            pltpu.VMEM((DEPTH, cols), jnp.bfloat16),
            pltpu.VMEM((DEPTH, cols), jnp.bfloat16),
            pltpu.VMEM((2, HALF, 128), jnp.float32),
            pltpu.VMEM((2, HALF, 128), jnp.float32),
            pltpu.VMEM((2, 1, cols), jnp.float32),
            pltpu.VMEM((pairs, 2, 1, cols), jnp.float32),
            pltpu.VMEM((count, cols), jnp.float32),
            dma((views, 3)),
            dma((views, 3)),
            dma((views, 2)),
            dma((views, 2)),
            dma((4,)),
            dma,
            dma((pairs, 2, disps)),
            dma((2, slots)),
        ],
        compiler_params=pltpu.CompilerParams(
            collective_id=0, has_side_effects=True, vmem_limit_bytes=62 * 1000 * 1000
        ),
        name="match",
    )(image, sharpness, paired, offset, row_range)


def settle_kernel(left_ref, right_ref, left_out, right_out, held, sems):
    sides = ((left_ref, left_out), (right_ref, right_out))
    slots = left_ref.shape[0]
    inward = [[pltpu.make_async_copy(source.at[slot], held.at[side, slot], sems.at[0, side, slot]) for slot in range(slots)] for side, (source, target) in enumerate(sides)]
    outward = [[pltpu.make_async_copy(held.at[side, slot], target.at[slot], sems.at[1, side, slot]) for slot in range(slots)] for side, (source, target) in enumerate(sides)]
    for group in inward:
        for copy in group:
            copy.start()
    for ahead, after in zip(inward, outward):
        for first, second in zip(ahead, after):
            first.wait()
            second.start()
    for group in outward:
        for copy in group:
            copy.wait()


def settle(left, right):
    anywhere = pl.BlockSpec(memory_space=pl.ANY)
    return pl.pallas_call(
        settle_kernel,
        out_shape=(left, right),
        in_specs=[anywhere] * 2,
        out_specs=(anywhere, anywhere),
        scratch_shapes=[pltpu.VMEM((2, *left.shape), jnp.float32), pltpu.SemaphoreType.DMA((2, 2, left.shape[0]))],
        compiler_params=pltpu.CompilerParams(vmem_limit_bytes=62 * 1000 * 1000),
        name="settle",
    )(left, right)


def shards(images, sharpness, paired, offset, row_range):
    left, right = match(images[0], sharpness[None], paired, offset, row_range)
    left, right = settle(left, right)
    return (left[None], right[None])


def solution(mesh):
    return jax.shard_map(
        shards,
        mesh=mesh,
        in_specs=(
            P("view", "row", None),
            P("view"),
            P("view", None),
            P("view", None),
            P("view", None, None),
        ),
        out_specs=(P("view", None, "row", None), P("view", None, "row", None)),
        check_vma=False,
    )
```

```python
import functools
import math

import jax
import jax.numpy as jnp
from jax import lax
from jax.experimental import pallas as pl
from jax.experimental.pallas import tpu as pltpu
from jax.sharding import PartitionSpec as P

DISP = 256
RAD = 4
TAPS = 2 * RAD + 1
EPSILON = 1e-05
DEPTH = 256
PAD = 128
BLOCK = 256
GRAIN = 16
MARGIN = 384
SPAN = 2 * BLOCK
HALF = 3 * 128
EXTRA = DEPTH - GRAIN


def rounded(value):
    return value.astype(jnp.bfloat16).astype(jnp.float32)


def split3(value):
    high = rounded(value)
    middle = rounded(value - high)
    return (high, middle, value - high - middle)


def row_of(view, disp, row_count):
    group = lax.axis_size("view") * lax.axis_size("disp")
    return (view * lax.axis_size("disp") + disp) * row_count // group


def segments(row, row_count):
    found = []
    for delta in (-1, 0, 1):
        low = max(row - RAD, delta * row_count)
        high = min(row + RAD + 1, (delta + 1) * row_count)
        for begin, end in ((low, min(high, row + RAD)), (max(low, row + RAD), high)):
            if end > begin:
                found.append((delta, begin - delta * row_count, end - begin, begin - row + RAD))
    return found


def tiled(row, width):
    return jnp.concatenate([row] * (width // 128), axis=1)


def emit(values, end, order, mark, cols_ref):
    for index, value in enumerate(values):
        high = value.astype(jnp.bfloat16)
        parts = (high, (value - high.astype(jnp.float32)).astype(jnp.bfloat16))
        for group in range(3):
            start = (group * len(values) + index) * GRAIN
            cols_ref[start : start + GRAIN, :] = parts[order[group]]
    high = rounded(end)
    parts = (high, end - high)
    place = lax.broadcasted_iota(jnp.int32, (GRAIN, end.shape[1]), 0)
    rest = mark
    for group in range(3):
        rest = jnp.where(place == group, parts[order[group]], rest)
    cols_ref[EXTRA:DEPTH, :] = rest.astype(jnp.bfloat16)


def build(window_ref, gain, left_refs, right_refs):
    cols = window_ref.shape[1] - 2 * PAD
    sub = lax.broadcasted_iota(jnp.int32, (GRAIN, 128), 0)
    lane = lax.broadcasted_iota(jnp.int32, (GRAIN, DEPTH), 1) - EXTRA
    main = window_ref[0:8, :]
    last = window_ref[8:9, :]
    taps = [main[:, PAD - RAD + tap : PAD - RAD + tap + cols] for tap in range(TAPS)]
    fan = pltpu.roll(jnp.broadcast_to(last, main.shape), 0, 1, stride=1, stride_axis=0)
    taps.append(fan[:, PAD - RAD + 7 : PAD - RAD + 7 + cols])
    end = last[:, PAD + RAD : PAD + RAD + cols]
    values = [jnp.concatenate(taps[index : index + 2], axis=0) for index in range(0, TAPS + 1, 2)]
    width = main.shape[1]
    sub8 = lax.broadcasted_iota(jnp.int32, main.shape, 0)
    sums = jnp.sum(main, axis=0, keepdims=True) + last
    squares = jnp.sum(main * main, axis=0, keepdims=True) + last * last
    total = jnp.where(sub8 < 4, sums, squares)
    double = total + pltpu.roll(total, width - 1, 1)
    double = double + pltpu.roll(double, width - 2, 1)
    double = double + pltpu.roll(double, width - 4, 1)
    total = double + pltpu.roll(total, width - 8, 1)
    total = total[:, PAD - RAD : PAD - RAD + cols] * (1.0 / (TAPS * TAPS))
    mean = total[0:1]
    var = total[4:5] - mean * mean
    values = [value - mean for value in values]
    end = end - mean
    scale = lax.rsqrt(var + EPSILON) * (1.0 / TAPS)
    zero = jnp.zeros((GRAIN, 128), jnp.float32)
    if right_refs is not None:
        cols_ref, rows_ref = right_refs
        mark = jnp.where((sub >= 6) & (sub < 9), 1.0, zero)
        emit([value * scale for value in values], end * scale, (0, 0, 1), tiled(mark, cols), cols_ref)
        rows_ref[MARGIN : MARGIN + cols, :] = cols_ref[...].T
        flag = jnp.where((lane >= 3) & (lane < 9), 1.0, 0.0).astype(jnp.bfloat16)
        rows_ref[0:MARGIN, :] = jnp.concatenate([flag] * (MARGIN // GRAIN), axis=0)
    if left_refs is not None:
        cols_ref, rows_ref = left_refs
        floor = [-part for part in split3(jnp.broadcast_to(gain, (GRAIN, 128)))]
        mark = zero
        for place in range(3):
            mark = jnp.where(sub == 3 + place, floor[place], mark)
        scale = scale * tiled(gain, cols)
        emit([value * scale for value in values], end * scale, (0, 1, 0), tiled(mark, cols), cols_ref)
        rows_ref[0:cols, :] = cols_ref[...].T
        edge = jnp.zeros((GRAIN, DEPTH), jnp.float32)
        for place in range(6):
            edge = jnp.where(lane == 3 + place, tiled(floor[place % 3], DEPTH), edge)
        rows_ref[cols : cols + MARGIN, :] = jnp.concatenate([edge.astype(jnp.bfloat16)] * (MARGIN // GRAIN), axis=0)


def turned(tiles, amount, forward):
    lane = lax.broadcasted_iota(jnp.int32, tiles[0].shape, 1)
    count = len(tiles)
    if forward:
        moved = [pltpu.roll(tile, amount, 1) for tile in tiles]
        return [jnp.where(lane < amount, moved[index - 1], moved[index]) for index in range(count)]
    moved = [pltpu.roll(tile, (128 - amount) & 127, 1) for tile in tiles]
    return [jnp.where(lane < 128 - amount, moved[index], moved[(index + 1) % count]) for index in range(count)]


class Turn:
    def __init__(self, source_ref, target_ref, amount, forward):
        self.source, self.target, self.forward = source_ref, target_ref, forward
        self.amount = amount if forward else (128 - amount) & 127
        self.edge = amount if forward else 128 - amount
        self.moved = {}
        size = EXTRA // 3
        self.parts = [(0, size), (2 * size, DEPTH)] if forward else [(0, 2 * size), (EXTRA, DEPTH)]
        self.copy = size if forward else 2 * size

    def tile(self, index, part):
        if (index, part) not in self.moved:
            begin, end = part
            self.moved[index, part] = pltpu.roll(self.source[begin:end, index * 128 : index * 128 + 128], self.amount, 1)
        return self.moved[index, part]

    def block(self, block):
        count = self.source.shape[1] // 128
        wide = BLOCK // 128
        size = EXTRA // 3
        for index in range(block * wide, block * wide + wide):
            place = slice(index * 128, index * 128 + 128)
            for part in self.parts:
                begin, end = part
                lane = lax.broadcasted_iota(jnp.int32, (end - begin, 128), 1)
                if self.forward:
                    tile = jnp.where(lane < self.edge, self.tile(max(index - 1, 0), part), self.tile(index, part))
                else:
                    tile = jnp.where(lane < self.edge, self.tile(index, part), self.tile(min(index + 1, count - 1), part))
                self.target[begin:end, place] = tile
                if begin == 0:
                    self.target[self.copy : self.copy + size, place] = tile[0:size]


def soft_half(score_ref, result_ref, column, left):
    lane = lax.broadcasted_iota(jnp.int32, (8, 128), 1)
    sub = lax.broadcasted_iota(jnp.int32, (8, 128), 0)
    skew = lane - sub
    sub_f = sub.astype(jnp.float32)
    lane_f = lane[0:1].astype(jnp.float32)
    slack = 0 if left else 1
    steps = DISP // 8
    corner = 128 // 8

    def load(step):
        return score_ref[8 * step : 8 * step + 8, :]

    near = [skew < 8 * step + slack for step in range(corner)]
    scores = [jnp.where(near[step], load(step), load(step + steps)) for step in range(corner)]
    scores += [load(step) for step in range(corner, steps)]
    tops = scores[:4]
    for step in range(4, steps):
        tops[step % 4] = jnp.maximum(tops[step % 4], scores[step])
    top = jnp.maximum(jnp.maximum(tops[0], tops[1]), jnp.maximum(tops[2], tops[3]))
    top = jnp.broadcast_to(jnp.max(top, axis=0, keepdims=True), (8, 128))
    zero = jnp.zeros((8, 128), jnp.float32)
    summed, running, far = ([zero, zero], [zero, zero], [zero, zero])
    for step in range(steps):
        weight = jnp.exp2(scores[step] - top)
        if step < corner:
            far[step % 2] = far[step % 2] + jnp.where(near[step], 0.0, weight)
        summed[step % 2] = summed[step % 2] + weight
        running[step % 2] = running[step % 2] + summed[step % 2]
    both = summed[0] + summed[1]
    moment = 8.0 * (steps * both - 2.0 * (running[0] + running[1]) + summed[1])
    moment = moment + sub_f * both + float(DISP) * (far[0] + far[1])
    total = jnp.sum(both, axis=0, keepdims=True)
    moment = jnp.sum(moment, axis=0, keepdims=True)
    if left:
        weighted = (lane_f + DISP) * total - moment
    else:
        weighted = moment - lane_f * total
    result_ref[:, column : column + 128] = weighted / (total * DISP)


def soft_pair(
    left_cols, left_rows, right_cols, right_rows, left_turned, right_turned, left_score, right_score, raw,
    left_result, right_result, coarse, fine, keep,
):
    cols = left_cols.shape[1]
    count = cols // BLOCK
    left_turn = Turn(left_cols, left_turned, fine, False)
    right_turn = Turn(right_cols, right_turned, fine, True)

    def scores(rows_ref, row_start, cols_ref, block, score_ref):
        score = jnp.dot(
            rows_ref[pl.ds(row_start * GRAIN, SPAN), :],
            cols_ref[:, block * BLOCK : (block + 1) * BLOCK],
            preferred_element_type=jnp.float32,
        )
        score_ref[0] = score[0:HALF, 0:128]
        score_ref[1] = score[128 : 128 + HALF, 128:256]

    def left_scores(block):
        scores(right_rows, block * (BLOCK // GRAIN) + (MARGIN - BLOCK) // GRAIN - coarse, left_turned, block, left_score)

    def right_scores(block):
        scores(left_rows, block * (BLOCK // GRAIN) + coarse, right_turned, block, right_score)

    def soft(score_ref, side, block, left):
        for half in range(2):
            soft_half(score_ref.at[half], raw.at[side], block * BLOCK + half * 128, left)

    left_turn.block(0)
    left_scores(0)
    right_turn.block(0)
    for block in range(count):
        if block + 1 < count:
            left_turn.block(block + 1)
            right_turn.block(block + 1)
        right_scores(block)
        soft(left_score, 0, block, True)
        if block + 1 < count:
            left_scores(block + 1)
        soft(right_score, 1, block, False)

    even = (DISP - 1) / (2.0 * DISP)
    lane = lax.broadcasted_iota(jnp.int32, (1, 128), 1)
    for side, result_ref in enumerate((left_result, right_result)):
        tiles = [jnp.broadcast_to(raw[side, :, start : start + 128], (8, 128)) for start in range(0, cols, 128)]
        tiles = [tile[0:1] for tile in turned(tiles, fine, side == 0)]
        if side == 0:
            tiles[0] = jnp.where(lane < fine, even, tiles[0])
        else:
            tiles[-1] = jnp.where(lane >= 128 - fine, even, tiles[-1])
        for index, tile in enumerate(tiles):
            result_ref[:, index * 128 : index * 128 + 128] = tile * keep


def place_of(view, row, disp):
    return dict(device_id={"view": view, "row": row, "disp": disp}, device_id_type=pl.DeviceIdType.MESH)


def signal(view, row, disp):
    pl.semaphore_signal(pltpu.get_barrier_semaphore(), inc=1, **place_of(view, row, disp))


def match_kernel(
    slots, image_ref, sharp_hbm, paired_hbm, offset_hbm, range_hbm, left_ref, right_ref,
    sharp_ref, paired_ref, offset_ref, range_ref, window, ints, floats, int_table,
    left_cols, left_rows, right_cols, right_rows, left_turned, right_turned, left_score, right_score, raw, result, empty,
    window_send, window_recv, meta_send, meta_recv, scalar_sem, table_sem, result_send, result_recv,
):
    count, cols = image_ref.shape
    views, bands, disps = (lax.axis_size(axis) for axis in ("view", "row", "disp"))
    view, band, disp = (lax.axis_index(axis) for axis in ("view", "row", "disp"))
    group = views * disps
    share = group // count
    member = view * disps + disp
    mine = row_of(view, disp, count)
    sends = member % share == 0
    rows_of = [sorted({row_of(other, place, count) for place in range(disps)}) for other in range(views)]

    scalars = [
        pltpu.make_async_copy(source, target, scalar_sem.at[index])
        for index, (source, target) in enumerate(
            ((sharp_hbm, sharp_ref), (paired_hbm, paired_ref), (offset_hbm, offset_ref), (range_hbm, range_ref))
        )
    ]
    for copy in scalars:
        copy.start()
    for start in (0, PAD + cols):
        window[:, :, start : start + PAD] = jnp.zeros((views, 16, PAD), jnp.float32)

    @pl.when(((mine < RAD) & (band == 0)) | ((mine + RAD >= count) & (band == bands - 1)))
    def _():
        window[...] = jnp.zeros_like(window)


    def inside(row):
        return (row >= 0) & (row < bands)

    for other in range(views):
        for place in range(disps):

            @pl.when((view != other) | (disp != place))
            def _():
                signal(other, band, place)

    expected = group - 1
    for delta in (-1, 1):
        needs = False
        wanted = 0
        for row in range(count):
            has = any(part[0] == delta for part in segments(row, count))
            needs = needs | ((mine == row) & has)
        for other in range(views):
            for row in rows_of[other]:
                if any(part[0] == delta for part in segments(row, count)):
                    wanted = wanted + jnp.where(row_of(other, disp, count) == row, 1, 0)

        @pl.when(needs & inside(band + delta))
        def _():
            for other in range(views):
                signal(other, band + delta, disp)

        expected = expected + jnp.where(inside(band - delta), wanted, 0)
    empty[...] = jnp.zeros_like(empty)

    def clearing(step):
        for side in range(2):
            for slot in range(slots):
                other = view + slot + 1 if side == 0 else view - slot - 1

                @pl.when((other < 0) | (other >= views))
                def _():
                    step(pltpu.make_async_copy(empty, (left_ref, right_ref)[side].at[slot], result_recv.at[side, slot]))

    clearing(lambda copy: copy.start())

    for copy in scalars:
        copy.wait()
    for slot in range(slots):

        def fill(kind, value):
            ints[view, kind * slots + slot : kind * slots + slot + 1] = value

        shift = jnp.broadcast_to(offset_ref[0:1, slot : slot + 1], (1, 128))
        fill(0, jnp.broadcast_to(paired_ref[0:1, slot : slot + 1], (1, 128)))
        fill(1, shift >> GRAIN.bit_length() - 1)
        fill(2, shift & (GRAIN - 1))
        for end in range(2):
            fill(3 + end, jnp.broadcast_to(range_ref[0, slot : slot + 1, end : end + 1], (1, 128)))
    floats[view] = jnp.broadcast_to(sharp_ref[...], (8, 128))
    pl.semaphore_wait(pltpu.get_barrier_semaphore(), expected)

    def window_copy(source, part, index, other, target_band):
        delta, begin, length, place = part
        return pltpu.make_async_remote_copy(
            src_ref=image_ref.at[pl.ds(begin, length)],
            dst_ref=window.at[source, pl.ds(place, length), pl.ds(PAD, cols)],
            send_sem=window_send.at[other, index],
            recv_sem=window_recv.at[source, index],
            **place_of(other, target_band, disp),
        )

    def own_copy(source, part, index):
        delta, begin, length, place = part
        return pltpu.make_async_copy(
            image_ref.at[pl.ds(begin, length)],
            window.at[source, pl.ds(place, length), pl.ds(PAD, cols)],
            window_recv.at[source, index],
        )

    def meta_copies(source, other):
        return [
            pltpu.make_async_remote_copy(
                src_ref=ref.at[source], dst_ref=ref.at[source],
                send_sem=meta_send.at[other, index], recv_sem=meta_recv.at[source, index],
                **place_of(other, band, disp),
            )
            for index, ref in enumerate((ints, floats))
        ]

    def sending(step, local):
        for other in range(views):

            @pl.when(view != other)
            def _():
                for copy in meta_copies(view, other):
                    step(copy)

            for row in rows_of[other]:

                @pl.when(row_of(other, disp, count) == row)
                def _():
                    for index, part in enumerate(segments(row, count)):
                        if part[0] != 0:

                            @pl.when(inside(band - part[0]))
                            def _():
                                step(window_copy(view, part, index, other, band - part[0]))

                    @pl.when(view != other)
                    def _():
                        for index, part in enumerate(segments(row, count)):
                            if part[0] == 0:
                                step(window_copy(view, part, index, other, band))

                    if local:

                        @pl.when(view == other)
                        def _():
                            for index, part in enumerate(segments(row, count)):
                                if part[0] == 0:
                                    own_copy(view, part, index).start()

    sending(lambda copy: copy.start(), True)

    for other in range(views):

        @pl.when(view != other)
        def _():
            for copy in meta_copies(other, other):
                copy.wait_recv()

    table = pltpu.make_async_copy(ints, int_table, table_sem)
    table.start()

    def arrive(source):
        for row in range(count):

            @pl.when(mine == row)
            def _():
                for index, part in enumerate(segments(row, count)):
                    if part[0] == 0:
                        own_copy(source, part, index).wait()
                    else:
                        pl.when(inside(band + part[0]))(own_copy(source, part, index).wait)

    for source in range(views):
        arrive(source)
        build(
            window.at[source], floats[source, 0:1, :] * math.log2(math.e),
            (left_cols.at[source], left_rows.at[source]) if source < views - 1 else None,
            (right_cols.at[source - 1], right_rows.at[source - 1]) if source > 0 else None,
        )
    table.wait()

    pairs = [(first, slot) for first in range(views - 1) for slot in range(min(slots, views - 1 - first))]

    def outcome(index, first, slot, side, place):
        target = first + side * (slot + 1)
        out = (left_ref, right_ref)[side].at[slot, pl.ds(mine, 1)]
        source = result.at[index, side]
        away = lambda: pltpu.make_async_remote_copy(
            src_ref=source, dst_ref=out,
            send_sem=result_send.at[index, side, place], recv_sem=result_recv.at[side, slot],
            **place_of(target, band, place),
        )
        home = lambda: pltpu.make_async_copy(source, out, result_recv.at[side, slot])
        return target, (away, home)

    def spread(index, first, slot, start):
        for side in range(2):
            for place in range(disps):
                target, (away, home) = outcome(index, first, slot, side, place)
                own = (target == view) & (disp == place)

                @pl.when(sends & jnp.logical_not(own))
                def _():
                    if start:
                        away().start()
                    else:
                        away().wait_send()

                if start:

                    @pl.when(sends & own)
                    def _():
                        home().start()

    def find(index):
        first = sum(jnp.where(index == at, pair[0], 0) for at, pair in enumerate(pairs))
        slot = sum(jnp.where(index == at, pair[1], 0) for at, pair in enumerate(pairs))
        return first, slot

    line = band * count + mine

    def match_pair(index, carry):
        first, slot = find(index)
        partner = first + slot + 1
        begin, end, pairing = (ints[first, pl.ds(kind * slots + slot, 1), :] for kind in (3, 4, 0))
        keep = jnp.where((begin <= line) & (end > line), pairing, 0).astype(jnp.float32)
        soft_pair(
            left_cols.at[first], left_rows.at[first], right_cols.at[partner - 1], right_rows.at[partner - 1],
            left_turned, right_turned, left_score, right_score, raw, result.at[index, 0], result.at[index, 1],
            int_table[first, slots + slot, 0], int_table[first, 2 * slots + slot, 0], keep,
        )
        spread(index, first, slot, True)
        return carry

    lax.fori_loop(0, len(pairs), match_pair, 0)

    sending(lambda copy: copy.wait_send(), False)
    for index, (first, slot) in enumerate(pairs):
        spread(index, first, slot, False)
    clearing(lambda copy: copy.wait())
    for side in range(2):
        for slot in range(slots):
            other = view + slot + 1 if side == 0 else view - slot - 1

            @pl.when((other >= 0) & (other < views))
            def _():
                out = (left_ref, right_ref)[side].at[slot]
                pltpu.make_async_copy(out, out, result_recv.at[side, slot]).wait()


def match(image, sharpness, paired, offset, row_range):
    views, disps = (lax.axis_size(axis) for axis in ("view", "disp"))
    count, cols = image.shape
    slots = paired.shape[1]
    pairs = sum(min(slots, views - 1 - first) for first in range(views - 1))
    entries = -(-5 * slots // 8) * 8
    anywhere = pl.BlockSpec(memory_space=pl.ANY)
    out = jax.ShapeDtypeStruct((slots, count, cols), jnp.float32)
    dma = pltpu.SemaphoreType.DMA
    return pl.pallas_call(
        functools.partial(match_kernel, slots),
        out_shape=(out, out),
        in_specs=[anywhere] * 5,
        out_specs=(anywhere, anywhere),
        scratch_shapes=[
            pltpu.VMEM(sharpness.shape, jnp.float32),
            pltpu.VMEM(paired.shape, jnp.int32),
            pltpu.VMEM(offset.shape, jnp.int32),
            pltpu.VMEM(row_range.shape, jnp.int32),
            pltpu.VMEM((views, 16, cols + 2 * PAD), jnp.float32),
            pltpu.VMEM((views, entries, 128), jnp.int32),
            pltpu.VMEM((views, 8, 128), jnp.float32),
            pltpu.SMEM((views, entries, 128), jnp.int32),
            pltpu.VMEM((views - 1, DEPTH, cols), jnp.bfloat16),
            pltpu.VMEM((views - 1, cols + MARGIN, DEPTH), jnp.bfloat16),
            pltpu.VMEM((views - 1, DEPTH, cols), jnp.bfloat16),
            pltpu.VMEM((views - 1, cols + MARGIN, DEPTH), jnp.bfloat16),
            pltpu.VMEM((DEPTH, cols), jnp.bfloat16),
            pltpu.VMEM((DEPTH, cols), jnp.bfloat16),
            pltpu.VMEM((2, HALF, 128), jnp.float32),
            pltpu.VMEM((2, HALF, 128), jnp.float32),
            pltpu.VMEM((2, 1, cols), jnp.float32),
            pltpu.VMEM((pairs, 2, 1, cols), jnp.float32),
            pltpu.VMEM((count, cols), jnp.float32),
            dma((views, 3)),
            dma((views, 3)),
            dma((views, 2)),
            dma((views, 2)),
            dma((4,)),
            dma,
            dma((pairs, 2, disps)),
            dma((2, slots)),
        ],
        compiler_params=pltpu.CompilerParams(
            collective_id=0, has_side_effects=True, vmem_limit_bytes=62 * 1000 * 1000
        ),
        name="match",
    )(image, sharpness, paired, offset, row_range)


def settle_kernel(left_ref, right_ref, left_out, right_out, held, sems):
    sides = ((left_ref, left_out), (right_ref, right_out))
    slots = left_ref.shape[0]
    inward = [[pltpu.make_async_copy(source.at[slot], held.at[side, slot], sems.at[0, side, slot]) for slot in range(slots)] for side, (source, target) in enumerate(sides)]
    outward = [[pltpu.make_async_copy(held.at[side, slot], target.at[slot], sems.at[1, side, slot]) for slot in range(slots)] for side, (source, target) in enumerate(sides)]
    for group in inward:
        for copy in group:
            copy.start()
    for ahead, after in zip(inward, outward):
        for first, second in zip(ahead, after):
            first.wait()
            second.start()
    for group in outward:
        for copy in group:
            copy.wait()


def settle(left, right):
    anywhere = pl.BlockSpec(memory_space=pl.ANY)
    return pl.pallas_call(
        settle_kernel,
        out_shape=(left, right),
        in_specs=[anywhere] * 2,
        out_specs=(anywhere, anywhere),
        scratch_shapes=[pltpu.VMEM((2, *left.shape), jnp.float32), pltpu.SemaphoreType.DMA((2, 2, left.shape[0]))],
        compiler_params=pltpu.CompilerParams(vmem_limit_bytes=62 * 1000 * 1000),
        name="settle",
    )(left, right)


def shards(images, sharpness, paired, offset, row_range):
    left, right = match(images[0], sharpness[None], paired, offset, row_range)
    left, right = settle(left, right)
    return (left[None], right[None])


def solution(mesh):
    return jax.shard_map(
        shards,
        mesh=mesh,
        in_specs=(
            P("view", "row", None),
            P("view"),
            P("view", None),
            P("view", None),
            P("view", None, None),
        ),
        out_specs=(P("view", None, "row", None), P("view", None, "row", None)),
        check_vma=False,
    )
```
